512 devices in a mesh: out: 32 (over z, y_lo, core), inp: 16 (over x, y_hi).
Axes of the slice: x: 4, y: 8 (y_hi: 4, y_lo: 2; y = y_hi * 2 + y_lo), z: 8, core: 2. Of those that a mesh axis runs over, the one named last changes fastest.
Arguments:
- grads: bfloat16 [1024, 8192], P('out', 'inp'), may hold values from -6 to 6
- acts: bfloat16 [1024, 28672], P('inp', 'out'), may hold values from -6 to 6
- grad_basis: bfloat16 [8192, 8192], P('inp', 'out'), may hold values from -0.0625 to 0.0625
- act_basis: bfloat16 [28672, 14336], P('out', 'inp'), may hold values from -0.03125 to 0.03125
Outputs:
- eigenvalues: float32 [8192, 14336], P('out', 'inp')
The draws below stay inside these ranges and needn't reach their ends.
All inputs are finite; a program needn't handle non-finite values.
Results may differ from the reference program's by a relative error of at most 0.0041.
Values may be sent and summed in bfloat16 or wider, within the bound.
No kernel may reach another device: no remote copies, remote signals or barrier semaphores. Data moves between devices by JAX's collectives and lax.ppermute only.
A program may use at most 64 MiB of HBM per device.

```python
import jax
import jax.numpy as jnp

D = 8192
FF = 28672
EIG = 14336
SEQS = 2
SEQ_LEN = 512
TOKENS = 1024


def levels(rng, extent, cuts, smallest, high):
    loudness, own = 1.0, jax.random.fold_in(rng, 6)
    for position, blocks in cuts:
        draws = jnp.exp(jax.random.uniform(jax.random.fold_in(own, position), (blocks,), jnp.float32, smallest / len(cuts), high / len(cuts)))
        loudness = loudness * jnp.repeat(draws, extent[position] // blocks).reshape([-1 if axis == position else 1 for axis in range(len(extent))])
    return loudness


def bell_draw(rng, dims, deviation, most, shards=(), kind=jnp.bfloat16):
    gain = levels(rng, dims, shards, -0.22, 0.18) if shards else 1.0
    entries = jax.random.normal(rng, dims, jnp.float32) * deviation * gain
    return jnp.minimum(jnp.maximum(entries, -most), most).astype(kind)


def setup_inputs(seed: int = 0) -> dict:
    keys = jax.random.split(jax.random.key(seed), 5)
    return {
        "grads": bell_draw(keys[0], (TOKENS, D), 1.0, 6.0, ((0, 32), (1, 16))),
        "acts": bell_draw(keys[1], (TOKENS, FF), 1.0, 6.0, ((0, 16), (1, 32))),
        "grad_basis": bell_draw(keys[2], (D, D), D ** -0.5, 0.0625, ((0, 16), (1, 32))),
        "act_basis": bell_draw(keys[3], (FF, EIG), FF ** -0.5, 0.03125, ((0, 32), (1, 16))),
    }


def reference(grads, acts, grad_basis, act_basis):
    grad_rot = jnp.dot(grads, grad_basis, preferred_element_type=jnp.float32).astype(jnp.bfloat16)
    act_rot = jnp.dot(acts, act_basis, preferred_element_type=jnp.float32).astype(jnp.bfloat16)
    total = jnp.zeros((grad_rot.shape[1], act_rot.shape[1]), jnp.float32)
    for seq_index in range(SEQS):
        lower = seq_index * SEQ_LEN
        rotated = jnp.dot(grad_rot[lower:lower + SEQ_LEN].T, act_rot[lower:lower + SEQ_LEN], preferred_element_type=jnp.float32)
        total = total + rotated * rotated
    return total / (SEQS * SEQ_LEN)
```

```python
import jax
import jax.numpy as jnp
from jax import lax
from jax.experimental import pallas as pl
from jax.experimental.pallas import tpu as pltpu
from jax.sharding import Mesh, PartitionSpec as P

SEQS = 2
SEQ_LEN = 512
OUT = ("z", "ylo", "core")
INP = ("x", "yhi")
CHIPS = ("z", "ylo")
BF16 = jnp.bfloat16
F32 = jnp.float32
VMEM = pl.BlockSpec(memory_space=pltpu.VMEM)


def kernel_call(body, shapes, args, flops=0):
    moved = sum(a.size * a.dtype.itemsize for a in args) + sum(s.size * s.dtype.itemsize for s in shapes)
    many = len(shapes) > 1
    return pl.pallas_call(
        body,
        out_shape=shapes if many else shapes[0],
        in_specs=[VMEM] * len(args),
        out_specs=[VMEM] * len(shapes) if many else VMEM,
        compiler_params=pltpu.CompilerParams(vmem_limit_bytes=40 * 2**20),
        cost_estimate=pl.CostEstimate(flops=flops, bytes_accessed=moved, transcendentals=0),
    )(*args)


def swap(value, axis, flip):
    size = lax.axis_size(axis)
    return lax.ppermute(value, axis, [(s, s ^ flip) for s in range(size)])


def stack_kernel(*refs):
    blocks, outs, row = refs[:4], refs[4:], 0
    for block in blocks:
        height = outs[0].shape[0]
        outs[row // height][row % height:row % height + block.shape[0], :] = block[...]
        row += block.shape[0]


def gather_yhi(mine, parts):
    blocks = [mine, swap(mine, "yhi", 1), swap(mine, "yhi", 2), swap(mine, "yhi", 3)]
    rows, columns = mine.shape
    shapes = [jax.ShapeDtypeStruct((4 * rows // parts, columns), mine.dtype)] * parts
    return kernel_call(stack_kernel, shapes, blocks)


def gather_chips(copies):
    return lax.all_to_all(copies, CHIPS, 0, 0, tiled=True)


def act_dot_kernel(top, bottom, top1, bottom1, top2, bottom2, top3, bottom3, own, other, out):
    features = own.shape[0]
    for pair in range(4):
        first, second = ((top, bottom), (top1, bottom1), (top2, bottom2), (top3, bottom3))[pair]
        rows = jnp.concatenate([first[...], second[...]])
        total = jnp.dot(rows[:, :features], own[...], preferred_element_type=F32)
        total += jnp.dot(rows[:, features:], other[...], preferred_element_type=F32)
        block = out.shape[1]
        for part in range(rows.shape[0] // block):
            at = pair * (rows.shape[0] // block) + part
            out[at] = total[part * block:(part + 1) * block].astype(BF16)


def sum_copies_kernel(parts, out):
    total = parts[0].astype(F32)
    for index in range(1, parts.shape[0]):
        total += parts[index].astype(F32)
    rounded = total.astype(BF16)
    for index in range(out.shape[0]):
        out[index] = rounded


def sum_split_kernel(parts, mine, give):
    total = parts[0].astype(F32)
    for index in range(1, parts.shape[0]):
        total += parts[index].astype(F32)
    rounded = total.astype(BF16)
    columns = mine.shape[1]
    mine[...] = rounded[:, :columns]
    give[...] = rounded[:, columns:]


def square_kernel(g0, g1, g2, g3, act_mine, act_theirs, out):
    columns = out.shape[0]
    half = act_mine.shape[0] // SEQS
    grads = (jnp.concatenate([g0[...], g1[...]]), jnp.concatenate([g2[...], g3[...]]))
    total = 0.0
    for seq in range(SEQS):
        rows = slice(seq * half, (seq + 1) * half)
        contract = (((0,), (0,)), ((), ()))
        rotated = lax.dot_general(grads[seq][:, :columns], act_mine[rows, :], contract, preferred_element_type=F32)
        rotated += lax.dot_general(grads[seq][:, columns:], act_theirs[rows, :], contract, preferred_element_type=F32)
        total = total + rotated * rotated
    out[...] = total * (1.0 / (SEQS * SEQ_LEN))


def shards(grads, acts, grad_basis, act_basis):
    core = lax.axis_index("core")
    half = acts.shape[0] // 2
    keep = lax.dynamic_slice_in_dim(acts, core * half, half)
    give = lax.dynamic_slice_in_dim(acts, (1 - core) * half, half)
    act_own = jnp.concatenate([keep, swap(give, "core", 1)], axis=1)
    act_basis_other = swap(act_basis, "core", 1)
    grad_basis_both = jnp.concatenate([grad_basis, swap(grad_basis, "core", 1)], axis=1)

    top, bottom = gather_yhi(act_own, 2)
    top3, bottom1 = swap(top, "x", 3), swap(bottom, "x", 1)
    bottom3, top1 = swap(bottom, "x", 3), swap(top, "x", 1)
    top2, bottom2 = swap(top3, "x", 1), swap(bottom1, "x", 3)

    rows = grads.shape[0]
    grad_rows = gather_chips(jnp.broadcast_to(grads[None], (16, *grads.shape)))
    grad_partial = jnp.dot(
        grad_rows.reshape(16 * rows, -1), grad_basis_both, preferred_element_type=F32
    ).astype(BF16)
    grad_parts = lax.all_to_all(grad_partial.reshape(16, rows, -1), INP, 0, 0, tiled=True)
    columns = grad_basis.shape[1]
    narrow = jax.ShapeDtypeStruct((rows, columns), BF16)
    grad_mine, grad_give = kernel_call(sum_split_kernel, [narrow, narrow], [grad_parts])
    grad_own = jnp.concatenate([grad_mine, swap(grad_give, "core", 1)], axis=1)
    top2, bottom2, grad_own = lax.optimization_barrier((top2, bottom2, grad_own))
    g0 = gather_yhi(grad_own, 1)

    tokens, eig = 16 * half, act_basis.shape[1]
    blocks = jax.ShapeDtypeStruct((16, half, eig), BF16)
    act_partial = kernel_call(
        act_dot_kernel,
        [blocks],
        [top, bottom, top1, bottom1, top2, bottom2, top3, bottom3, act_basis, act_basis_other],
        flops=2 * tokens * 2 * act_basis.shape[0] * eig,
    )
    act_parts = lax.all_to_all(act_partial, CHIPS, 0, 0, tiled=True)
    act_parts, g0 = lax.optimization_barrier((act_parts, g0))
    g1, g2, g3 = swap(g0, "x", 1), swap(g0, "x", 2), swap(g0, "x", 3)
    act_mine = gather_chips(kernel_call(sum_copies_kernel, [blocks], [act_parts])).reshape(tokens, eig)
    act_theirs = swap(act_mine, "core", 1)

    return kernel_call(
        square_kernel,
        [jax.ShapeDtypeStruct((columns, eig), F32)],
        [g0, g1, g2, g3, act_mine, act_theirs],
        flops=2 * 2 * tokens * columns * eig,
    )


def solution(mesh):
    split = Mesh(mesh.devices.reshape(8, 2, 2, 4, 4), OUT + INP)
    return jax.shard_map(
        shards,
        mesh=split,
        in_specs=(P(OUT, INP), P(INP, OUT), P(INP, OUT), P(OUT, INP)),
        out_specs=P(OUT, INP),
        check_vma=False,
    )
```

```python
import jax
import jax.numpy as jnp
from jax import lax
from jax.experimental import pallas as pl
from jax.experimental.pallas import tpu as pltpu
from jax.sharding import Mesh, PartitionSpec as P

SEQS = 2
SEQ_LEN = 512
OUT = ("z", "ylo", "core")
INP = ("x", "yhi")
CHIPS = ("z", "ylo")
BF16 = jnp.bfloat16
F32 = jnp.float32
VMEM = pl.BlockSpec(memory_space=pltpu.VMEM)


def kernel_call(body, shapes, args, flops=0):
    moved = sum(a.size * a.dtype.itemsize for a in args) + sum(s.size * s.dtype.itemsize for s in shapes)
    many = len(shapes) > 1
    return pl.pallas_call(
        body,
        out_shape=shapes if many else shapes[0],
        in_specs=[VMEM] * len(args),
        out_specs=[VMEM] * len(shapes) if many else VMEM,
        compiler_params=pltpu.CompilerParams(vmem_limit_bytes=40 * 2**20),
        cost_estimate=pl.CostEstimate(flops=flops, bytes_accessed=moved, transcendentals=0),
    )(*args)


def swap(value, axis, flip):
    size = lax.axis_size(axis)
    return lax.ppermute(value, axis, [(s, s ^ flip) for s in range(size)])


def dot_kernel(*refs):
    pieces, (basis0, basis1, out) = refs[:4], refs[4:]
    features = basis0.shape[0]
    blocks, block = out.shape[0], out.shape[1]
    each = blocks // 4
    total = 0.0
    for core, basis in ((0, basis0), (1, basis1)):
        rows = jnp.concatenate([piece[core * each:(core + 1) * each] for piece in pieces])
        total += jnp.dot(rows.reshape(blocks * block, features), basis[...], preferred_element_type=F32)
    out[...] = total.astype(BF16).reshape(out.shape)


def sum_parts(parts):
    total = parts[0].astype(F32)
    for index in range(1, parts.shape[0]):
        total += parts[index].astype(F32)
    return total.astype(BF16)


def sum_copies_kernel(parts, out):
    rounded = sum_parts(parts)
    for index in range(out.shape[0]):
        out[index] = rounded


def sum_split_kernel(parts, out):
    rounded = sum_parts(parts)
    copies, columns = out.shape[0] // 2, out.shape[2]
    for index in range(out.shape[0]):
        core = index // copies
        out[index] = rounded[:, core * columns:(core + 1) * columns]


def square_kernel(grad_mine, grad_theirs, act_mine, act_theirs, out):
    half = act_mine.shape[0] // SEQS
    total = 0.0
    for seq in range(SEQS):
        rows = slice(seq * half, (seq + 1) * half)
        contract = (((0,), (0,)), ((), ()))
        rotated = lax.dot_general(grad_mine[rows, :], act_mine[rows, :], contract, preferred_element_type=F32)
        rotated += lax.dot_general(grad_theirs[rows, :], act_theirs[rows, :], contract, preferred_element_type=F32)
        total = total + rotated * rotated
    out[...] = total * (1.0 / (SEQS * SEQ_LEN))


def both_cores(core, own):
    other = swap(own, "core", 1)
    return jnp.where(core == 0, own, other), jnp.where(core == 0, other, own)


def shards(grads, acts, grad_basis, act_basis):
    core, x = lax.axis_index("core"), lax.axis_index("x")
    half, features = acts.shape[0] // 2, acts.shape[1]
    tokens, eig = 16 * half, act_basis.shape[1]
    rows, columns = grads.shape[0], grad_basis.shape[1]

    copies = jnp.broadcast_to(acts.reshape(2, 1, half, features), (2, 4, half, features))
    act0 = lax.all_to_all(copies.reshape(8, half, features), ("core", "yhi"), 0, 0, tiled=True)
    act_basis0, act_basis1 = both_cores(core, act_basis)
    grad_basis_both = jnp.concatenate(both_cores(core, grad_basis), axis=1)

    act0, grads = lax.optimization_barrier((act0, grads))
    act1, act3, act2 = swap(act0, "x", 1), swap(act0, "x", 3), swap(act0, "x", 2)
    grad_copies = jnp.broadcast_to(grads[None], (16, *grads.shape))
    grad_rows = lax.all_to_all(grad_copies, CHIPS, 0, 0, tiled=True)

    blocks = jax.ShapeDtypeStruct((16, half, eig), BF16)
    act_partial = kernel_call(
        dot_kernel,
        [blocks],
        [act0, act1, act2, act3, act_basis0, act_basis1],
        flops=2 * tokens * 2 * features * eig,
    )
    act_partial, grad_rows = lax.optimization_barrier((act_partial, grad_rows))
    act_parts = lax.all_to_all(act_partial, CHIPS, 0, 0, tiled=True)
    grad_partial = jnp.dot(
        grad_rows.reshape(16 * rows, -1), grad_basis_both, preferred_element_type=F32
    ).astype(BF16)
    grad_parts = lax.all_to_all(grad_partial.reshape(16, rows, -1), INP, 0, 0, tiled=True)

    act_copies = kernel_call(sum_copies_kernel, [blocks], [act_parts])
    act_copies, grad_parts = lax.optimization_barrier((act_copies, grad_parts))
    act_mine = lax.all_to_all(act_copies, CHIPS, 0, 0, tiled=True).reshape(tokens, eig)
    split = jax.ShapeDtypeStruct((32, rows, columns), BF16)
    grad_split = kernel_call(sum_split_kernel, [split], [grad_parts])
    grad_all = lax.all_to_all(grad_split, ("core", *INP), 0, 0, tiled=True).reshape(2, 4, 4 * rows, columns)
    grad_mine, grad_theirs = (
        jnp.concatenate([grad_all[core ^ other, x ^ flip] for flip in range(4)]) for other in range(2)
    )
    act_theirs = swap(act_mine, "core", 1)

    return kernel_call(
        square_kernel,
        [jax.ShapeDtypeStruct((columns, eig), F32)],
        [grad_mine, grad_theirs, act_mine, act_theirs],
        flops=2 * 2 * tokens * columns * eig,
    )


def solution(mesh):
    split = Mesh(mesh.devices.reshape(8, 2, 2, 4, 4), OUT + INP)
    return jax.shard_map(
        shards,
        mesh=split,
        in_specs=(P(OUT, INP), P(INP, OUT), P(INP, OUT), P(OUT, INP)),
        out_specs=P(OUT, INP),
        check_vma=False,
    )
```

```python
import jax
import jax.numpy as jnp
from jax import lax
from jax.experimental import pallas as pl
from jax.experimental.pallas import tpu as pltpu
from jax.sharding import Mesh, PartitionSpec as P

SEQS = 2
SEQ_LEN = 512
OUT = ("z", "ylo", "core")
INP = ("x", "yhi")
CHIPS = ("z", "ylo")
BF16 = jnp.bfloat16
F32 = jnp.float32
VMEM = pl.BlockSpec(memory_space=pltpu.VMEM)


def kernel_call(body, shapes, args, flops=0):
    moved = sum(a.size * a.dtype.itemsize for a in args) + sum(s.size * s.dtype.itemsize for s in shapes)
    many = len(shapes) > 1
    return pl.pallas_call(
        body,
        out_shape=shapes if many else shapes[0],
        in_specs=[VMEM] * len(args),
        out_specs=[VMEM] * len(shapes) if many else VMEM,
        compiler_params=pltpu.CompilerParams(vmem_limit_bytes=40 * 2**20),
        cost_estimate=pl.CostEstimate(flops=flops, bytes_accessed=moved, transcendentals=0),
    )(*args)


def swap(value, axis, flip):
    size = lax.axis_size(axis)
    return lax.ppermute(value, axis, [(s, s ^ flip) for s in range(size)])


def dot_kernel(act0, act1, low2, high2, act3, basis0, basis1, out, done):
    features = basis0.shape[0]
    blocks, block = out.shape[0], out.shape[1]
    each = blocks // 4
    first = [act0[:each], act1[:each], low2[...], act3[:each]]
    second = [act0[each:], act1[each:], high2[...], act3[each:]]
    total = 0.0
    for pieces, basis in ((first, basis0), (second, basis1)):
        rows = jnp.concatenate(pieces).reshape(blocks * block, features)
        total += jnp.dot(rows, basis[...], preferred_element_type=F32)
    out[...] = total.astype(BF16).reshape(out.shape)
    done[...] = jnp.zeros_like(done)


def grad_dot_kernel(done, rows, own, other, out):
    columns = own.shape[1]
    out[:, :columns] = jnp.dot(rows[...], own[...], preferred_element_type=F32)
    out[:, columns:] = jnp.dot(rows[...], other[...], preferred_element_type=F32)


def sum_kernel(parts, out):
    total = parts[0].astype(F32)
    for index in range(1, parts.shape[0]):
        total += parts[index].astype(F32)
    out[...] = total.astype(BF16)


def square_kernel(grad_mine, grad_theirs, act_mine, act_theirs, out):
    half = act_mine.shape[0] // SEQS
    total = 0.0
    for seq in range(SEQS):
        rows = slice(seq * half, (seq + 1) * half)
        contract = (((0,), (0,)), ((), ()))
        rotated = lax.dot_general(grad_mine[rows, :], act_mine[rows, :], contract, preferred_element_type=F32)
        rotated += lax.dot_general(grad_theirs[rows, :], act_theirs[rows, :], contract, preferred_element_type=F32)
        total = total + rotated * rotated
    out[...] = total * (1.0 / (SEQS * SEQ_LEN))


def both(index, axis, own):
    other = swap(own, axis, 1)
    return jnp.where(index == 0, own, other), jnp.where(index == 0, other, own)


def shards(grads, acts, grad_basis, act_basis):
    core, ylo, x = lax.axis_index("core"), lax.axis_index("ylo"), lax.axis_index("x")
    half, features = acts.shape[0] // 2, acts.shape[1]
    tokens, eig = 16 * half, act_basis.shape[1]
    columns = grad_basis.shape[1]

    copies = jnp.broadcast_to(acts.reshape(2, 1, half, features), (2, 4, half, features))
    act0 = lax.all_to_all(copies.reshape(8, half, features), ("core", "yhi"), 0, 0, tiled=True)
    act_basis0, act_basis1 = both(core, "core", act_basis)
    grad_basis_other = swap(grad_basis, "core", 1)
    grad_rows = lax.all_gather(lax.all_gather(grads, "ylo", axis=0, tiled=True), "z", axis=0, tiled=True)

    act1, act3 = swap(act0, "x", 1), swap(act0, "x", 3)
    low2, high2 = swap(act3[:4], "x", 1), swap(act1[4:], "x", 3)

    blocks = jax.ShapeDtypeStruct((16, half, eig), BF16)
    act_partial, done = kernel_call(
        dot_kernel,
        [blocks, jax.ShapeDtypeStruct((8, 128), F32)],
        [act0, act1, low2, high2, act3, act_basis0, act_basis1],
        flops=2 * tokens * 2 * features * eig,
    )
    act_parts = lax.all_to_all(act_partial, CHIPS, 0, 0, tiled=True)

    grad_partial = kernel_call(
        grad_dot_kernel,
        [jax.ShapeDtypeStruct((tokens, 2 * columns), F32)],
        [done, grad_rows, grad_basis, grad_basis_other],
        flops=2 * tokens * grads.shape[1] * 2 * columns,
    )
    grad_sum = lax.psum_scatter(grad_partial, "x", scatter_dimension=0, tiled=True)
    grad_sum = lax.psum_scatter(grad_sum, "yhi", scatter_dimension=0, tiled=True).astype(BF16)

    act_sum = kernel_call(sum_kernel, [jax.ShapeDtypeStruct((half, eig), BF16)], [act_parts])
    act_pair = jnp.concatenate(both(ylo, "ylo", act_sum))
    act_mine = lax.all_gather(act_pair, "z", axis=0, tiled=True)

    grad_all = lax.all_gather(lax.all_gather(grad_sum, "yhi", axis=0, tiled=True), "x", axis=0, tiled=True)
    grad_all = grad_all.reshape(4, tokens // 4, 2 * columns)
    grad_all = jnp.concatenate([grad_all[x ^ flip] for flip in range(4)])
    grad_mine, grad_theirs = grad_all[:, :columns], swap(grad_all[:, columns:], "core", 1)
    act_theirs = swap(act_mine, "core", 1)

    return kernel_call(
        square_kernel,
        [jax.ShapeDtypeStruct((columns, eig), F32)],
        [grad_mine, grad_theirs, act_mine, act_theirs],
        flops=2 * 2 * tokens * columns * eig,
    )


def solution(mesh):
    split = Mesh(mesh.devices.reshape(8, 2, 2, 4, 4), OUT + INP)
    return jax.shard_map(
        shards,
        mesh=split,
        in_specs=(P(OUT, INP), P(INP, OUT), P(INP, OUT), P(OUT, INP)),
        out_specs=P(OUT, INP),
        check_vma=False,
    )
```

```python
import jax
import jax.numpy as jnp
from jax import lax
from jax.experimental import pallas as pl
from jax.experimental.pallas import tpu as pltpu
from jax.sharding import Mesh, PartitionSpec as P

SEQS = 2
SEQ_LEN = 512
OUT = ("z", "ylo", "core")
INP = ("x", "yhi")
CHIPS = ("z", "ylo")
BF16 = jnp.bfloat16
F32 = jnp.float32
VMEM = pl.BlockSpec(memory_space=pltpu.VMEM)


def kernel_call(body, shapes, args, flops=0):
    moved = sum(a.size * a.dtype.itemsize for a in args) + sum(s.size * s.dtype.itemsize for s in shapes)
    many = len(shapes) > 1
    return pl.pallas_call(
        body,
        out_shape=shapes if many else shapes[0],
        in_specs=[VMEM] * len(args),
        out_specs=[VMEM] * len(shapes) if many else VMEM,
        compiler_params=pltpu.CompilerParams(vmem_limit_bytes=40 * 2**20),
        cost_estimate=pl.CostEstimate(flops=flops, bytes_accessed=moved, transcendentals=0),
    )(*args)


def swap(value, axis, flip):
    size = lax.axis_size(axis)
    return lax.ppermute(value, axis, [(s, s ^ flip) for s in range(size)])


def stack_kernel(*refs):
    blocks, out, done, row = refs[:-2], refs[-2], refs[-1], 0
    for block in blocks:
        out[row:row + block.shape[0], :] = block[...]
        row += block.shape[0]
    done[...] = jnp.zeros_like(done)


def gather_yhi(mine):
    blocks = [mine, swap(mine, "yhi", 1), swap(mine, "yhi", 2), swap(mine, "yhi", 3)]
    rows, columns = mine.shape
    shapes = [jax.ShapeDtypeStruct((4 * rows, columns), mine.dtype), jax.ShapeDtypeStruct((8, 128), F32)]
    return kernel_call(stack_kernel, shapes, blocks)


def act_dot_kernel(act0, act1, low2, high2, act3, own, other, out, done):
    features = own.shape[0]
    rows = jnp.concatenate([act0[...], act1[...], low2[...], high2[...], act3[...]])
    total = jnp.dot(rows[:, :features], own[...], preferred_element_type=F32)
    total += jnp.dot(rows[:, features:], other[...], preferred_element_type=F32)
    out[...] = total.astype(BF16).reshape(out.shape)
    done[...] = jnp.zeros_like(done)


def grad_dot_kernel(done, rows, own, other, out):
    columns = own.shape[1]
    total = jnp.concatenate(
        [jnp.dot(rows[...], basis[...], preferred_element_type=F32) for basis in (own, other)], axis=1
    )
    out[...] = total.astype(BF16).reshape(out.shape)


def sum_parts(parts):
    total = parts[0].astype(F32)
    for index in range(1, parts.shape[0]):
        total += parts[index].astype(F32)
    return total.astype(BF16)


def sum_copies_kernel(parts, out):
    rounded = sum_parts(parts)
    for index in range(out.shape[0]):
        out[index] = rounded


def sum_split_kernel(done, parts, mine, give):
    rounded = sum_parts(parts)
    columns = mine.shape[1]
    mine[...] = rounded[:, :columns]
    give[...] = rounded[:, columns:]


def square_kernel(g0, g1, g2, g3, act_mine, act_theirs, out):
    columns = out.shape[0]
    half = act_mine.shape[0] // SEQS
    grads = (jnp.concatenate([g0[...], g1[...]]), jnp.concatenate([g2[...], g3[...]]))
    total = 0.0
    for seq in range(SEQS):
        rows = slice(seq * half, (seq + 1) * half)
        contract = (((0,), (0,)), ((), ()))
        rotated = lax.dot_general(grads[seq][:, :columns], act_mine[rows, :], contract, preferred_element_type=F32)
        rotated += lax.dot_general(grads[seq][:, columns:], act_theirs[rows, :], contract, preferred_element_type=F32)
        total = total + rotated * rotated
    out[...] = total * (1.0 / (SEQS * SEQ_LEN))


def shards(grads, acts, grad_basis, act_basis):
    core = lax.axis_index("core")
    half, features = acts.shape[0] // 2, acts.shape[1]
    tokens, eig = 16 * half, act_basis.shape[1]
    rows, columns = grads.shape[0], grad_basis.shape[1]

    keep = lax.dynamic_slice_in_dim(acts, core * half, half)
    give = lax.dynamic_slice_in_dim(acts, (1 - core) * half, half)
    act_own = jnp.concatenate([keep, swap(give, "core", 1)], axis=1)
    act_basis_other = swap(act_basis, "core", 1)
    grad_basis_other = swap(grad_basis, "core", 1)

    act0, done = gather_yhi(act_own)
    act1, act3 = swap(act0, "x", 1), swap(act0, "x", 3)
    low2, high2 = swap(act3[:2 * half], "x", 1), swap(act1[2 * half:], "x", 3)

    grad_copies = jnp.broadcast_to(grads[None], (16, *grads.shape))
    grad_rows = lax.all_to_all(grad_copies, CHIPS, 0, 0, tiled=True).reshape(tokens, -1)
    grad_partial = kernel_call(
        grad_dot_kernel,
        [jax.ShapeDtypeStruct((16, rows, 2 * columns), BF16)],
        [done, grad_rows, grad_basis, grad_basis_other],
        flops=2 * tokens * grads.shape[1] * 2 * columns,
    )
    grad_parts = lax.all_to_all(grad_partial, INP, 0, 0, tiled=True)

    blocks = jax.ShapeDtypeStruct((16, half, eig), BF16)
    act_partial, done = kernel_call(
        act_dot_kernel,
        [blocks, jax.ShapeDtypeStruct((8, 128), F32)],
        [act0, act1, low2, high2, act3, act_basis, act_basis_other],
        flops=2 * tokens * 2 * features * eig,
    )
    act_parts = lax.all_to_all(act_partial, CHIPS, 0, 0, tiled=True)

    narrow = jax.ShapeDtypeStruct((rows, columns), BF16)
    grad_mine, grad_give = kernel_call(sum_split_kernel, [narrow, narrow], [done, grad_parts])
    grad_own = jnp.concatenate([grad_mine, swap(grad_give, "core", 1)], axis=1)
    g0, _ = gather_yhi(grad_own)
    act_parts, g0 = lax.optimization_barrier((act_parts, g0))

    act_mine = lax.all_to_all(kernel_call(sum_copies_kernel, [blocks], [act_parts]), CHIPS, 0, 0, tiled=True)
    g1, g2, g3 = swap(g0, "x", 1), swap(g0, "x", 2), swap(g0, "x", 3)
    act_mine, g1, g2, g3 = lax.optimization_barrier((act_mine.reshape(tokens, eig), g1, g2, g3))
    act_theirs = swap(act_mine, "core", 1)

    return kernel_call(
        square_kernel,
        [jax.ShapeDtypeStruct((columns, eig), F32)],
        [g0, g1, g2, g3, act_mine, act_theirs],
        flops=2 * 2 * tokens * columns * eig,
    )


def solution(mesh):
    split = Mesh(mesh.devices.reshape(8, 2, 2, 4, 4), OUT + INP)
    return jax.shard_map(
        shards,
        mesh=split,
        in_specs=(P(OUT, INP), P(INP, OUT), P(INP, OUT), P(OUT, INP)),
        out_specs=P(OUT, INP),
        check_vma=False,
    )
```

```python
import jax
import jax.numpy as jnp
from jax import lax
from jax.experimental import pallas as pl
from jax.experimental.pallas import tpu as pltpu
from jax.sharding import Mesh, PartitionSpec as P

SEQS = 2
SEQ_LEN = 512
OUT = ("z", "ylo", "core")
INP = ("x", "yhi")
CHIPS = ("z", "ylo")
BF16 = jnp.bfloat16
F32 = jnp.float32
VMEM = pl.BlockSpec(memory_space=pltpu.VMEM)
SMEM = pl.BlockSpec(memory_space=pltpu.SMEM)
ANY = pl.BlockSpec(memory_space=pl.ANY)


def kernel_call(body, shapes, args, flops=0, scalars=0, unread=0):
    moved = sum(a.size * a.dtype.itemsize for a in args) + sum(s.size * s.dtype.itemsize for s in shapes)
    many = len(shapes) > 1
    return pl.pallas_call(
        body,
        out_shape=shapes if many else shapes[0],
        in_specs=[SMEM] * scalars + [VMEM] * (len(args) - scalars - unread) + [ANY] * unread,
        out_specs=[VMEM] * len(shapes) if many else VMEM,
        compiler_params=pltpu.CompilerParams(vmem_limit_bytes=40 * 2**20),
        cost_estimate=pl.CostEstimate(flops=flops, bytes_accessed=moved, transcendentals=0),
    )(*args)


def swap(value, axis, flip):
    size = lax.axis_size(axis)
    return lax.ppermute(value, axis, [(s, s ^ flip) for s in range(size)])


def act_dot_kernel(acts, basis0, basis1, order, out):
    blocks, block = out.shape[0], out.shape[1]
    total = 0.0
    for core, basis in ((0, basis0), (1, basis1)):
        rows = jnp.concatenate([acts[2 * x + core] for x in range(4)])
        total += jnp.dot(rows, basis[...], preferred_element_type=F32)
    out[...] = total.astype(BF16).reshape(out.shape)


def grad_dot_kernel(rows, own, other, out):
    columns = own.shape[1]
    blocks, block = out.shape[0], out.shape[1]
    for side, basis in ((0, own), (1, other)):
        part = jnp.dot(rows[...], basis[...], preferred_element_type=F32).astype(BF16)
        out[:, :, side * columns:(side + 1) * columns] = part.reshape(blocks, block, columns)


def sum_parts(parts):
    total = parts[0].astype(F32)
    for index in range(1, parts.shape[0]):
        total += parts[index].astype(F32)
    return total.astype(BF16)


def sum_copies_kernel(parts, out):
    rounded = sum_parts(parts)
    for index in range(out.shape[0]):
        out[index] = rounded


def split_kernel(at, parts, order, out):
    core = at[0]
    rounded = sum_parts(parts)
    copies, columns = out.shape[0] // 2, out.shape[2]
    for index in range(copies):
        out[core * copies + index] = rounded[:, :columns]
        out[(1 - core) * copies + index] = rounded[:, columns:]


def square_kernel(at, grads, act_mine, act_theirs, out):
    core = at[0]
    half = act_mine.shape[0] // SEQS
    total = 0.0
    for seq in range(SEQS):
        rotated = 0.0
        for side, act in ((core, act_mine), (1 - core, act_theirs)):
            rotated += lax.dot_general(
                grads[side, seq], act[seq * half:(seq + 1) * half, :], (((0,), (0,)), ((), ())),
                preferred_element_type=F32,
            )
        total = total + rotated * rotated
    out[...] = total * (1.0 / (SEQS * SEQ_LEN))


def both(index, axis, own):
    other = swap(own, axis, 1)
    return jnp.where(index == 0, own, other), jnp.where(index == 0, other, own)


def shards(grads, acts, grad_basis, act_basis):
    core = lax.axis_index("core")
    at = core.astype(jnp.int32).reshape(1)
    half, features = acts.shape[0] // 2, acts.shape[1]
    tokens, eig = 16 * half, act_basis.shape[1]
    rows, columns = grads.shape[0], grad_basis.shape[1]

    copies = jnp.broadcast_to(acts.reshape(2, 1, half, features), (2, 4, half, features))
    act_yhi = lax.all_to_all(copies.reshape(8, half, features), ("core", "yhi"), 0, 0, tiled=True)
    act_basis0, act_basis1 = both(core, "core", act_basis)
    grad_basis_other = swap(grad_basis, "core", 1)

    act_yhi, grads = lax.optimization_barrier((act_yhi, grads))
    act_rows = lax.all_gather(act_yhi.reshape(8 * half, features), "x", axis=0, tiled=True)
    grad_copies = jnp.broadcast_to(grads[None], (16, *grads.shape))
    grad_rows = lax.all_to_all(grad_copies, CHIPS, 0, 0, tiled=True).reshape(tokens, -1)
    grad_partial = kernel_call(
        grad_dot_kernel,
        [jax.ShapeDtypeStruct((16, rows, 2 * columns), BF16)],
        [grad_rows, grad_basis, grad_basis_other],
        flops=2 * tokens * grads.shape[1] * 2 * columns,
    )
    grad_parts = lax.all_to_all(grad_partial, INP, 0, 0, tiled=True)

    blocks = jax.ShapeDtypeStruct((16, half, eig), BF16)
    act_partial = kernel_call(
        act_dot_kernel,
        [blocks],
        [act_rows.reshape(8, 4 * half, features), act_basis0, act_basis1, grad_partial],
        flops=2 * tokens * 2 * features * eig,
        unread=1,
    )
    act_parts = lax.all_to_all(act_partial, CHIPS, 0, 0, tiled=True)
    act_copies = kernel_call(sum_copies_kernel, [blocks], [act_parts])
    act_mine = lax.all_to_all(act_copies, CHIPS, 0, 0, tiled=True).reshape(tokens, eig)
    act_theirs = swap(act_mine, "core", 1)

    split = kernel_call(
        split_kernel,
        [jax.ShapeDtypeStruct((32, rows, columns), BF16)],
        [at, grad_parts, act_mine],
        scalars=1,
        unread=1,
    )
    grad_all = lax.all_to_all(split, ("core", *INP), 0, 0, tiled=True).reshape(2, SEQS, 8 * rows, columns)

    return kernel_call(
        square_kernel,
        [jax.ShapeDtypeStruct((columns, eig), F32)],
        [at, grad_all, act_mine, act_theirs],
        flops=2 * 2 * tokens * columns * eig,
        scalars=1,
    )


def solution(mesh):
    split = Mesh(mesh.devices.reshape(8, 2, 2, 4, 4), OUT + INP)
    return jax.shard_map(
        shards,
        mesh=split,
        in_specs=(P(OUT, INP), P(INP, OUT), P(INP, OUT), P(OUT, INP)),
        out_specs=P(OUT, INP),
        check_vma=False,
    )
```

```python
import jax
import jax.numpy as jnp
from jax import lax
from jax.experimental import pallas as pl
from jax.experimental.pallas import tpu as pltpu
from jax.sharding import Mesh, PartitionSpec as P

SEQS = 2
SEQ_LEN = 512
OUT = ("z", "ylo", "core")
INP = ("x", "yhi")
CHIPS = ("z", "ylo")
BF16 = jnp.bfloat16
F32 = jnp.float32
VMEM = pl.BlockSpec(memory_space=pltpu.VMEM)
SMEM = pl.BlockSpec(memory_space=pltpu.SMEM)
ANY = pl.BlockSpec(memory_space=pl.ANY)


def kernel_call(body, shapes, args, flops=0, scalars=0, unread=0, scratch=()):
    moved = sum(a.size * a.dtype.itemsize for a in args) + sum(s.size * s.dtype.itemsize for s in shapes)
    many = len(shapes) > 1
    return pl.pallas_call(
        body,
        out_shape=shapes if many else shapes[0],
        in_specs=[SMEM] * scalars + [VMEM] * (len(args) - scalars - unread) + [ANY] * unread,
        out_specs=[VMEM] * len(shapes) if many else VMEM,
        scratch_shapes=[pltpu.VMEM(s.shape, s.dtype) for s in scratch],
        compiler_params=pltpu.CompilerParams(vmem_limit_bytes=40 * 2**20),
        cost_estimate=pl.CostEstimate(flops=flops, bytes_accessed=moved, transcendentals=0),
    )(*args)


def swap(value, axis, flip):
    size = lax.axis_size(axis)
    return lax.ppermute(value, axis, [(s, s ^ flip) for s in range(size)])


def act_dot_kernel(acts, basis0, basis1, out, done):
    blocks, block = out.shape[0], out.shape[1]
    total = 0.0
    for core, basis in ((0, basis0), (1, basis1)):
        rows = jnp.concatenate([acts[2 * x + core] for x in range(4)])
        total += jnp.dot(rows, basis[...], preferred_element_type=F32)
    out[...] = total.astype(BF16).reshape(out.shape)
    done[...] = jnp.zeros_like(done)


def grad_dot_kernel(at, rows, own, other, order, mine, give1, give2, give3):
    columns = own.shape[1]
    tokens = mine.shape[0]
    for flip, out in enumerate((mine, give1, give2, give3)):
        block = rows[pl.ds(pl.multiple_of((at[1] ^ flip) * tokens, tokens), tokens), :]
        for side, basis in ((0, own), (1, other)):
            part = jnp.dot(block, basis[...], preferred_element_type=F32)
            out[:, side * columns:(side + 1) * columns] = part.astype(out.dtype)


def sum_x_kernel(at, mine, got1, got2, got3, keep, give1, give2, give3, scratch):
    scratch[...] = mine[...] + got1[...].astype(F32) + got2[...].astype(F32) + got3[...].astype(F32)
    tokens = keep.shape[0]
    for flip, out in enumerate((keep, give1, give2, give3)):
        out[...] = scratch[pl.ds(pl.multiple_of((at[2] ^ flip) * tokens, tokens), tokens), :]


def sum_yhi_kernel(mine, got1, got2, got3, keep, give):
    rounded = (mine[...] + got1[...] + got2[...] + got3[...]).astype(BF16)
    columns = keep.shape[1]
    keep[...] = rounded[:, :columns]
    give[...] = rounded[:, columns:]


def stack_kernel(at, block0, block1, block2, block3, out):
    tokens = block0.shape[0]
    for flip, block in enumerate((block0, block1, block2, block3)):
        out[pl.ds(pl.multiple_of((at[2] ^ flip) * tokens, tokens), tokens), :] = block[...]


def sum_copies_kernel(parts, out):
    total = parts[0].astype(F32)
    for index in range(1, parts.shape[0]):
        total += parts[index].astype(F32)
    rounded = total.astype(BF16)
    for index in range(out.shape[0]):
        out[index] = rounded


def square_kernel(at, g0, g1, g2, g3, act_mine, act_theirs, out):
    columns = out.shape[0]
    quarter = act_mine.shape[0] // 4
    total = 0.0
    for pair in (((0, g0), (1, g1)), ((2, g2), (3, g3))):
        rotated = 0.0
        for flip, grad in pair:
            at_row = pl.multiple_of((at[1] ^ flip) * quarter, quarter)
            for side, act in ((0, act_mine), (1, act_theirs)):
                rotated += lax.dot_general(
                    grad[:, side * columns:(side + 1) * columns], act[pl.ds(at_row, quarter), :],
                    (((0,), (0,)), ((), ())), preferred_element_type=F32,
                )
        total = total + rotated * rotated
    out[...] = total * (1.0 / (SEQS * SEQ_LEN))


def both(index, axis, own):
    other = swap(own, axis, 1)
    return jnp.where(index == 0, own, other), jnp.where(index == 0, other, own)


def shards(grads, acts, grad_basis, act_basis):
    core, x, yhi = (lax.axis_index(axis) for axis in ("core", "x", "yhi"))
    at = jnp.stack([core, x, yhi]).astype(jnp.int32)
    half, features = acts.shape[0] // 2, acts.shape[1]
    tokens, eig = 16 * half, act_basis.shape[1]
    rows, columns = grads.shape[0], grad_basis.shape[1]
    shape = jax.ShapeDtypeStruct

    copies = jnp.broadcast_to(acts.reshape(2, 1, half, features), (2, 4, half, features))
    act_yhi = lax.all_to_all(copies.reshape(8, half, features), ("core", "yhi"), 0, 0, tiled=True)
    act_basis0, act_basis1 = both(core, "core", act_basis)
    grad_basis_other = swap(grad_basis, "core", 1)

    act_yhi, grads = lax.optimization_barrier((act_yhi, grads))
    act_rows = lax.all_gather(act_yhi.reshape(8 * half, features), "x", axis=0, tiled=True)
    grad_copies = jnp.broadcast_to(grads[None], (16, *grads.shape))
    grad_rows = lax.all_to_all(grad_copies, CHIPS, 0, 0, tiled=True).reshape(tokens, -1)

    blocks = shape((16, half, eig), BF16)
    act_partial, done = kernel_call(
        act_dot_kernel,
        [blocks, shape((8, 128), F32)],
        [act_rows.reshape(8, 4 * half, features), act_basis0, act_basis1],
        flops=2 * tokens * 2 * features * eig,
    )
    act_parts = lax.all_to_all(act_partial, CHIPS, 0, 0, tiled=True)

    sent, kept = shape((4 * rows, 2 * columns), BF16), shape((4 * rows, 2 * columns), F32)
    mine, *gives = kernel_call(
        grad_dot_kernel,
        [kept, sent, sent, sent],
        [at, grad_rows, grad_basis, grad_basis_other, done],
        flops=2 * tokens * grads.shape[1] * 2 * columns,
        scalars=1,
        unread=1,
    )
    got = [swap(give, "x", flip) for flip, give in zip((1, 2, 3), gives)]
    mine, *gives = kernel_call(
        sum_x_kernel, [shape((rows, 2 * columns), F32)] * 4, [at, mine, *got], scalars=1, scratch=[kept]
    )
    got = [swap(give, "yhi", flip) for flip, give in zip((1, 2, 3), gives)]
    narrow = shape((rows, columns), BF16)
    keep, give = kernel_call(sum_yhi_kernel, [narrow, narrow], [mine, *got])

    grad_own = jnp.concatenate([keep, swap(give, "core", 1)], axis=1)
    got = [swap(grad_own, "yhi", flip) for flip in (1, 2, 3)]
    g0 = kernel_call(stack_kernel, [sent], [at, grad_own, *got], scalars=1)
    g1, g2, g3 = swap(g0, "x", 1), swap(g0, "x", 2), swap(g0, "x", 3)

    act_copies = kernel_call(sum_copies_kernel, [blocks], [act_parts])
    act_mine = lax.all_to_all(act_copies, CHIPS, 0, 0, tiled=True).reshape(tokens, eig)
    act_mine, g1, g2, g3 = lax.optimization_barrier((act_mine, g1, g2, g3))
    act_theirs = swap(act_mine, "core", 1)

    return kernel_call(
        square_kernel,
        [shape((columns, eig), F32)],
        [at, g0, g1, g2, g3, act_mine, act_theirs],
        flops=2 * 2 * tokens * columns * eig,
        scalars=1,
    )


def solution(mesh):
    split = Mesh(mesh.devices.reshape(8, 2, 2, 4, 4), OUT + INP)
    return jax.shard_map(
        shards,
        mesh=split,
        in_specs=(P(OUT, INP), P(INP, OUT), P(INP, OUT), P(OUT, INP)),
        out_specs=P(OUT, INP),
        check_vma=False,
    )
```

```python
import functools

import jax
import jax.numpy as jnp
from jax import lax
from jax.experimental import pallas as pl
from jax.experimental.pallas import tpu as pltpu
from jax.sharding import Mesh, PartitionSpec as P

SEQS = 2
SEQ_LEN = 512
OUT = ("z", "ylo", "core")
INP = ("x", "yhi")
CHIPS = ("z", "ylo")
BF16 = jnp.bfloat16
F32 = jnp.float32
VMEM = pl.BlockSpec(memory_space=pltpu.VMEM)
SMEM = pl.BlockSpec(memory_space=pltpu.SMEM)
ANY = pl.BlockSpec(memory_space=pl.ANY)


def kernel_call(body, shapes, args, flops=0, scalars=0, unread=0, scratch=()):
    moved = sum(a.size * a.dtype.itemsize for a in args) + sum(s.size * s.dtype.itemsize for s in shapes)
    many = len(shapes) > 1
    return pl.pallas_call(
        body,
        out_shape=shapes if many else shapes[0],
        in_specs=[SMEM] * scalars + [VMEM] * (len(args) - scalars - unread) + [ANY] * unread,
        out_specs=[VMEM] * len(shapes) if many else VMEM,
        scratch_shapes=[pltpu.VMEM(s.shape, s.dtype) for s in scratch],
        compiler_params=pltpu.CompilerParams(vmem_limit_bytes=40 * 2**20),
        cost_estimate=pl.CostEstimate(flops=flops, bytes_accessed=moved, transcendentals=0),
    )(*args)


def swap(value, axis, flip):
    size = lax.axis_size(axis)
    return lax.ppermute(value, axis, [(s, s ^ flip) for s in range(size)])


def act_dot_kernel(acts, basis0, basis1, order, out, done):
    blocks, block = out.shape[0], out.shape[1]
    total = 0.0
    for core, basis in ((0, basis0), (1, basis1)):
        rows = jnp.concatenate([acts[2 * x + core] for x in range(4)])
        total += jnp.dot(rows, basis[...], preferred_element_type=F32)
    out[...] = total.astype(BF16).reshape(out.shape)
    done[...] = jnp.zeros_like(done)


CORE, X_LOW, X_HIGH, YHI_LOW, YHI_HIGH = range(5)


def half_rows(bit, ref, rows):
    return ref[pl.ds(pl.multiple_of(bit * rows, rows), rows), :]


def grad_dot_kernel(at, rows, own, other, keep, give):
    columns = own.shape[1]
    tokens = keep.shape[0]
    for bit, out in ((at[X_HIGH], keep), (1 - at[X_HIGH], give)):
        block = half_rows(bit, rows, tokens)
        for side, basis in ((0, own), (1, other)):
            part = jnp.dot(block, basis[...], preferred_element_type=F32)
            out[:, side * columns:(side + 1) * columns] = part.astype(out.dtype)


def sum_halves_kernel(which, at, mine, got, order, keep, give, total):
    total[...] = mine[...] + got[...].astype(F32)
    for bit, out in ((at[which], keep), (1 - at[which], give)):
        out[...] = half_rows(bit, total, out.shape[0]).astype(out.dtype)


def sum_columns_kernel(mine, got, keep, give):
    rounded = (mine[...] + got[...]).astype(BF16)
    columns = keep.shape[1]
    keep[...] = rounded[:, :columns]
    give[...] = rounded[:, columns:]


def pair_kernel(which, at, mine, got, order, out):
    rows = mine.shape[0]
    for bit, block in ((at[which], mine), (1 - at[which], got)):
        out[pl.ds(pl.multiple_of(bit * rows, rows), rows), :] = block[...]


def sum_copies_kernel(parts, order, out):
    total = parts[0].astype(F32)
    for index in range(1, parts.shape[0]):
        total += parts[index].astype(F32)
    rounded = total.astype(BF16)
    for index in range(out.shape[0]):
        out[index] = rounded


def square_kernel(at, grad_here, grad_far, act_mine, act_theirs, out):
    columns = out.shape[0]
    half = act_mine.shape[0] // SEQS
    total = 0.0
    for bit, grad in ((at[X_HIGH], grad_here), (1 - at[X_HIGH], grad_far)):
        rotated = 0.0
        for side, act in ((0, act_mine), (1, act_theirs)):
            rotated += lax.dot_general(
                grad[:, side * columns:(side + 1) * columns], half_rows(bit, act, half),
                (((0,), (0,)), ((), ())), preferred_element_type=F32,
            )
        total = total + rotated * rotated
    out[...] = total * (1.0 / (SEQS * SEQ_LEN))


def both(index, axis, own):
    other = swap(own, axis, 1)
    return jnp.where(index == 0, own, other), jnp.where(index == 0, other, own)


def shards(grads, acts, grad_basis, act_basis):
    core, x, yhi = (lax.axis_index(axis) for axis in ("core", "x", "yhi"))
    at = jnp.stack([core, x % 2, x // 2, yhi % 2, yhi // 2]).astype(jnp.int32)
    half, features = acts.shape[0] // 2, acts.shape[1]
    tokens, eig = 16 * half, act_basis.shape[1]
    rows, columns = grads.shape[0], grad_basis.shape[1]
    shape = jax.ShapeDtypeStruct

    copies = jnp.broadcast_to(acts.reshape(2, 1, half, features), (2, 4, half, features))
    act_yhi = lax.all_to_all(copies.reshape(8, half, features), ("core", "yhi"), 0, 0, tiled=True)
    act_basis0, act_basis1 = both(core, "core", act_basis)
    grad_basis_other = swap(grad_basis, "core", 1)

    act_yhi, grads = lax.optimization_barrier((act_yhi, grads))
    act_rows = lax.all_gather(act_yhi.reshape(8 * half, features), "x", axis=0, tiled=True)
    grad_copies = jnp.broadcast_to(grads[None], (16, *grads.shape))
    grad_rows = lax.all_to_all(grad_copies, CHIPS, 0, 0, tiled=True).reshape(tokens, -1)

    wide = lambda count, kind: shape((count * rows, 2 * columns), kind)
    mine, give = kernel_call(
        grad_dot_kernel,
        [wide(8, F32), wide(8, BF16)],
        [at, grad_rows, grad_basis, grad_basis_other],
        flops=2 * tokens * grads.shape[1] * 2 * columns,
        scalars=1,
    )

    blocks = shape((16, half, eig), BF16)
    act_partial, done = kernel_call(
        act_dot_kernel,
        [blocks, shape((8, 128), F32)],
        [act_rows.reshape(8, 4 * half, features), act_basis0, act_basis1, give],
        flops=2 * tokens * 2 * features * eig,
        unread=1,
    )
    act_parts = lax.all_to_all(act_partial, CHIPS, 0, 0, tiled=True)

    for axis, flip, which, count, kind in (("x", 3, X_LOW, 4, BF16), ("x", 1, YHI_HIGH, 2, F32), ("yhi", 3, YHI_LOW, 1, F32)):
        mine, give = kernel_call(
            functools.partial(sum_halves_kernel, which),
            [wide(count, F32), wide(count, kind)],
            [at, mine, swap(give, axis, flip), done],
            scalars=1,
            unread=1,
            scratch=[wide(2 * count, F32)],
        )
    narrow = shape((rows, columns), BF16)
    keep, send = kernel_call(sum_columns_kernel, [narrow, narrow], [mine, swap(give, "yhi", 1)])

    act_copies = kernel_call(sum_copies_kernel, [blocks], [act_parts, mine], unread=1)
    act_mine = lax.all_to_all(act_copies, CHIPS, 0, 0, tiled=True).reshape(tokens, eig)
    here = jnp.concatenate([keep, swap(send, "core", 1)], axis=1)
    for axis, flip, which, count in (("yhi", 1, YHI_LOW, 2), ("yhi", 3, YHI_HIGH, 4), ("x", 1, X_LOW, 8)):
        here = kernel_call(
            functools.partial(pair_kernel, which),
            [wide(count, BF16)],
            [at, here, swap(here, axis, flip), act_copies],
            scalars=1,
            unread=1,
        )
    act_mine, far = lax.optimization_barrier((act_mine, swap(here, "x", 3)))
    act_theirs = swap(act_mine, "core", 1)

    return kernel_call(
        square_kernel,
        [shape((columns, eig), F32)],
        [at, here, far, act_mine, act_theirs],
        flops=2 * 2 * tokens * columns * eig,
        scalars=1,
    )


def solution(mesh):
    split = Mesh(mesh.devices.reshape(8, 2, 2, 4, 4), OUT + INP)
    return jax.shard_map(
        shards,
        mesh=split,
        in_specs=(P(OUT, INP), P(INP, OUT), P(INP, OUT), P(OUT, INP)),
        out_specs=P(OUT, INP),
        check_vma=False,
    )
```

```python
import jax
import jax.numpy as jnp
from jax import lax
from jax.experimental import pallas as pl
from jax.experimental.pallas import tpu as pltpu
from jax.sharding import Mesh, PartitionSpec as P

SEQS = 2
SEQ_LEN = 512
OUT = ("z", "ylo", "core")
INP = ("x", "yhi")
CHIPS = ("z", "ylo")
BF16 = jnp.bfloat16
F32 = jnp.float32
SMEM = pl.BlockSpec(memory_space=pltpu.SMEM)
VMEM = pl.BlockSpec(memory_space=pltpu.VMEM)


def kernel_call(body, shapes, args, flops=0, scalars=0):
    moved = sum(a.size * a.dtype.itemsize for a in args) + sum(s.size * s.dtype.itemsize for s in shapes)
    many = len(shapes) > 1
    return pl.pallas_call(
        body,
        out_shape=shapes if many else shapes[0],
        in_specs=[SMEM] * scalars + [VMEM] * (len(args) - scalars),
        out_specs=[VMEM] * len(shapes) if many else VMEM,
        compiler_params=pltpu.CompilerParams(vmem_limit_bytes=40 * 2**20),
        cost_estimate=pl.CostEstimate(flops=flops, bytes_accessed=moved, transcendentals=0),
    )(*args)


def swap(value, axis, flip):
    size = lax.axis_size(axis)
    return lax.ppermute(value, axis, [(s, s ^ flip) for s in range(size)])


def stack_kernel(*refs):
    blocks, out, done, row = refs[:-2], refs[-2], refs[-1], 0
    for block in blocks:
        out[row:row + block.shape[0], :] = block[...]
        row += block.shape[0]
    done[...] = jnp.zeros_like(done)


def gather_yhi(mine):
    return [mine, swap(mine, "yhi", 1), swap(mine, "yhi", 2), swap(mine, "yhi", 3)]


def stack(blocks):
    rows, columns = blocks[0].shape
    shapes = [jax.ShapeDtypeStruct((len(blocks) * rows, columns), BF16), jax.ShapeDtypeStruct((8, 128), F32)]
    return kernel_call(stack_kernel, shapes, blocks)


def act_dot_kernel(at, acts, last0, last1, last2, last3, own, other, out, done):
    features = own.shape[0]
    total = 0.0
    for side, basis in ((0, own), (1, other)):
        rows = []
        for flip, last in enumerate((last0, last1, last2, last3)):
            rows += [ref[..., side * features:(side + 1) * features] for ref in (acts.at[at[0] ^ flip], last)]
        total += jnp.dot(jnp.concatenate(rows), basis[...], preferred_element_type=F32)
    out[...] = total.astype(BF16).reshape(out.shape)
    done[...] = jnp.zeros_like(done)


def grad_dot_kernel(done, rows, own, other, out):
    columns = own.shape[1]
    total = jnp.concatenate(
        [jnp.dot(rows[...], basis[...], preferred_element_type=F32) for basis in (own, other)], axis=1
    )
    out[...] = total.astype(BF16).reshape(out.shape)


def sum_parts(parts):
    total = parts[0].astype(F32)
    for index in range(1, parts.shape[0]):
        total += parts[index].astype(F32)
    return total.astype(BF16)


def sum_copies_kernel(parts, out):
    rounded = sum_parts(parts)
    for index in range(out.shape[0]):
        out[index] = rounded


def sum_split_kernel(done, parts, mine, give):
    rounded = sum_parts(parts)
    columns = mine.shape[1]
    mine[...] = rounded[:, :columns]
    give[...] = rounded[:, columns:]


def square_kernel(g0, g1, g2, g3, act_mine, act_theirs, out):
    columns = out.shape[0]
    half = act_mine.shape[0] // SEQS
    grads = (jnp.concatenate([g0[...], g1[...]]), jnp.concatenate([g2[...], g3[...]]))
    total = 0.0
    for seq in range(SEQS):
        rows = slice(seq * half, (seq + 1) * half)
        contract = (((0,), (0,)), ((), ()))
        rotated = lax.dot_general(grads[seq][:, :columns], act_mine[rows, :], contract, preferred_element_type=F32)
        rotated += lax.dot_general(grads[seq][:, columns:], act_theirs[rows, :], contract, preferred_element_type=F32)
        total = total + rotated * rotated
    out[...] = total * (1.0 / (SEQS * SEQ_LEN))


def shards(grads, acts, grad_basis, act_basis):
    core, x = lax.axis_index("core"), lax.axis_index("x").astype(jnp.int32).reshape(1)
    half, features = acts.shape[0] // 2, acts.shape[1]
    tokens, eig = 16 * half, act_basis.shape[1]
    rows, columns = grads.shape[0], grad_basis.shape[1]

    keep = lax.dynamic_slice_in_dim(acts, core * half, half)
    give = lax.dynamic_slice_in_dim(acts, (1 - core) * half, half)
    act_own = jnp.concatenate([keep, swap(give, "core", 1)], axis=1)
    act_basis_other = swap(act_basis, "core", 1)
    grad_basis_other = swap(grad_basis, "core", 1)

    *first, last = gather_yhi(act_own)
    act_first, done = stack(first)
    act_rows = lax.all_gather(act_first, "x")
    lasts = [last, swap(last, "x", 1), swap(last, "x", 2), swap(last, "x", 3)]

    grad_copies = jnp.broadcast_to(grads[None], (16, *grads.shape))
    grad_rows = lax.all_to_all(grad_copies, CHIPS, 0, 0, tiled=True).reshape(tokens, -1)
    grad_partial = kernel_call(
        grad_dot_kernel,
        [jax.ShapeDtypeStruct((16, rows, 2 * columns), BF16)],
        [done, grad_rows, grad_basis, grad_basis_other],
        flops=2 * tokens * grads.shape[1] * 2 * columns,
    )
    grad_parts = lax.all_to_all(grad_partial, INP, 0, 0, tiled=True)

    blocks = jax.ShapeDtypeStruct((16, half, eig), BF16)
    act_partial, done = kernel_call(
        act_dot_kernel,
        [blocks, jax.ShapeDtypeStruct((8, 128), F32)],
        [x, act_rows, *lasts, act_basis, act_basis_other],
        flops=2 * tokens * 2 * features * eig,
        scalars=1,
    )
    act_parts = lax.all_to_all(act_partial, CHIPS, 0, 0, tiled=True)

    narrow = jax.ShapeDtypeStruct((rows, columns), BF16)
    grad_mine, grad_give = kernel_call(sum_split_kernel, [narrow, narrow], [done, grad_parts])
    grad_own = jnp.concatenate([grad_mine, swap(grad_give, "core", 1)], axis=1)
    g0, _ = stack(gather_yhi(grad_own))
    act_parts, g0 = lax.optimization_barrier((act_parts, g0))

    act_mine = lax.all_to_all(kernel_call(sum_copies_kernel, [blocks], [act_parts]), CHIPS, 0, 0, tiled=True)
    g1, g2, g3 = swap(g0, "x", 1), swap(g0, "x", 2), swap(g0, "x", 3)
    act_mine, g1, g2, g3 = lax.optimization_barrier((act_mine.reshape(tokens, eig), g1, g2, g3))
    act_theirs = swap(act_mine, "core", 1)

    return kernel_call(
        square_kernel,
        [jax.ShapeDtypeStruct((columns, eig), F32)],
        [g0, g1, g2, g3, act_mine, act_theirs],
        flops=2 * 2 * tokens * columns * eig,
    )


def solution(mesh):
    split = Mesh(mesh.devices.reshape(8, 2, 2, 4, 4), OUT + INP)
    return jax.shard_map(
        shards,
        mesh=split,
        in_specs=(P(OUT, INP), P(INP, OUT), P(INP, OUT), P(OUT, INP)),
        out_specs=P(OUT, INP),
        check_vma=False,
    )
```

```python
import jax
import jax.numpy as jnp
from jax import lax
from jax.experimental import pallas as pl
from jax.experimental.pallas import tpu as pltpu
from jax.sharding import Mesh, PartitionSpec as P

SEQS = 2
SEQ_LEN = 512
OUT = ("z", "ylo", "core")
INP = ("x", "yhi")
CHIPS = ("z", "ylo")
BF16 = jnp.bfloat16
F32 = jnp.float32
SMEM = pl.BlockSpec(memory_space=pltpu.SMEM)
ANY = pl.BlockSpec(memory_space=pl.ANY)
VMEM = pl.BlockSpec(memory_space=pltpu.VMEM)


def kernel_call(body, shapes, args, flops=0, scalars=0, unread=0):
    moved = sum(a.size * a.dtype.itemsize for a in args) + sum(s.size * s.dtype.itemsize for s in shapes)
    many = len(shapes) > 1
    return pl.pallas_call(
        body,
        out_shape=shapes if many else shapes[0],
        in_specs=[SMEM] * scalars + [VMEM] * (len(args) - scalars - unread) + [ANY] * unread,
        out_specs=[VMEM] * len(shapes) if many else VMEM,
        compiler_params=pltpu.CompilerParams(vmem_limit_bytes=40 * 2**20),
        cost_estimate=pl.CostEstimate(flops=flops, bytes_accessed=moved, transcendentals=0),
    )(*args)


def swap(value, axis, flip):
    size = lax.axis_size(axis)
    return lax.ppermute(value, axis, [(s, s ^ flip) for s in range(size)])


def gather_yhi(mine):
    return [mine, swap(mine, "yhi", 1), swap(mine, "yhi", 2), swap(mine, "yhi", 3)]


def stack_acts_kernel(block0, block1, block2, block3, order, out, done):
    rows, features = block0.shape[0], out.shape[2]
    for index, block in enumerate((block0, block1, block2, block3)):
        for side in range(2):
            out[side, index * rows:(index + 1) * rows, :] = block[:, side * features:(side + 1) * features]
    done[...] = jnp.zeros_like(done)


def stack_kernel(block0, block1, block2, block3, out):
    rows = block0.shape[0]
    for index, block in enumerate((block0, block1, block2, block3)):
        out[index * rows:(index + 1) * rows, :] = block[...]


def place_kernel(x, block0, block1, block2, block3, out):
    rows = block0.shape[0]
    for flip, block in enumerate((block0, block1, block2, block3)):
        out[pl.ds(pl.multiple_of((x[0] ^ flip) * rows, rows), rows), :] = block[...]


def act_dot_kernel(acts, own, other, out, done):
    total = 0.0
    for side, basis in ((0, own), (1, other)):
        rows = jnp.concatenate([acts[x, side] for x in range(acts.shape[0])])
        total += jnp.dot(rows, basis[...], preferred_element_type=F32)
    out[...] = total.astype(BF16).reshape(out.shape)
    done[...] = jnp.zeros_like(done)


def grad_dot_kernel(done, rows, own, other, out):
    columns = own.shape[1]
    total = jnp.concatenate(
        [jnp.dot(rows[...], basis[...], preferred_element_type=F32) for basis in (own, other)], axis=1
    )
    out[...] = total.astype(BF16).reshape(out.shape)


def sum_parts(parts):
    total = parts[0].astype(F32)
    for index in range(1, parts.shape[0]):
        total += parts[index].astype(F32)
    return total.astype(BF16)


def sum_copies_kernel(parts, out):
    rounded = sum_parts(parts)
    for index in range(out.shape[0]):
        out[index] = rounded


def sum_split_kernel(done, parts, mine, give):
    rounded = sum_parts(parts)
    columns = mine.shape[1]
    mine[...] = rounded[:, :columns]
    give[...] = rounded[:, columns:]


def square_kernel(grads, act_mine, act_theirs, out):
    columns = out.shape[0]
    half = act_mine.shape[0] // SEQS
    total = 0.0
    for seq in range(SEQS):
        rows = slice(seq * half, (seq + 1) * half)
        rotated = 0.0
        for side, act in ((0, act_mine), (1, act_theirs)):
            rotated += lax.dot_general(
                grads[rows, side * columns:(side + 1) * columns], act[rows, :], (((0,), (0,)), ((), ())),
                preferred_element_type=F32,
            )
        total = total + rotated * rotated
    out[...] = total * (1.0 / (SEQS * SEQ_LEN))


def shards(grads, acts, grad_basis, act_basis):
    core, x = lax.axis_index("core"), lax.axis_index("x").astype(jnp.int32).reshape(1)
    half, features = acts.shape[0] // 2, acts.shape[1]
    tokens, eig = 16 * half, act_basis.shape[1]
    rows, columns = grads.shape[0], grad_basis.shape[1]

    keep = lax.dynamic_slice_in_dim(acts, core * half, half)
    give = lax.dynamic_slice_in_dim(acts, (1 - core) * half, half)
    act_own = jnp.concatenate([keep, swap(give, "core", 1)], axis=1)
    act_basis_other = swap(act_basis, "core", 1)
    grad_basis_other = swap(grad_basis, "core", 1)

    grad_copies = jnp.broadcast_to(grads[None], (16, *grads.shape))
    grad_rows = lax.all_to_all(grad_copies, CHIPS, 0, 0, tiled=True).reshape(tokens, -1)
    act_yhi, done = kernel_call(
        stack_acts_kernel,
        [jax.ShapeDtypeStruct((2, 4 * half, features), BF16), jax.ShapeDtypeStruct((8, 128), F32)],
        [*gather_yhi(act_own), grad_rows],
        unread=1,
    )
    act_rows = lax.all_gather(act_yhi, "x")

    grad_partial = kernel_call(
        grad_dot_kernel,
        [jax.ShapeDtypeStruct((16, rows, 2 * columns), BF16)],
        [done, grad_rows, grad_basis, grad_basis_other],
        flops=2 * tokens * grads.shape[1] * 2 * columns,
    )
    grad_parts = lax.all_to_all(grad_partial, INP, 0, 0, tiled=True)

    blocks = jax.ShapeDtypeStruct((16, half, eig), BF16)
    act_partial, done = kernel_call(
        act_dot_kernel,
        [blocks, jax.ShapeDtypeStruct((8, 128), F32)],
        [act_rows, act_basis, act_basis_other],
        flops=2 * tokens * 2 * features * eig,
    )
    act_parts = lax.all_to_all(act_partial, CHIPS, 0, 0, tiled=True)

    narrow = jax.ShapeDtypeStruct((rows, columns), BF16)
    grad_mine, grad_give = kernel_call(sum_split_kernel, [narrow, narrow], [done, grad_parts])
    grad_own = jnp.concatenate([grad_mine, swap(grad_give, "core", 1)], axis=1)
    g0 = kernel_call(stack_kernel, [jax.ShapeDtypeStruct((4 * rows, 2 * columns), BF16)], gather_yhi(grad_own))
    act_parts, g0 = lax.optimization_barrier((act_parts, g0))

    act_mine = lax.all_to_all(kernel_call(sum_copies_kernel, [blocks], [act_parts]), CHIPS, 0, 0, tiled=True)
    grad_blocks = [g0, swap(g0, "x", 1), swap(g0, "x", 2), swap(g0, "x", 3)]
    grad_all = kernel_call(
        place_kernel, [jax.ShapeDtypeStruct((tokens, 2 * columns), BF16)], [x, *grad_blocks], scalars=1
    )
    act_mine, grad_all = lax.optimization_barrier((act_mine.reshape(tokens, eig), grad_all))
    act_theirs = swap(act_mine, "core", 1)

    return kernel_call(
        square_kernel,
        [jax.ShapeDtypeStruct((columns, eig), F32)],
        [grad_all, act_mine, act_theirs],
        flops=2 * 2 * tokens * columns * eig,
    )


def solution(mesh):
    split = Mesh(mesh.devices.reshape(8, 2, 2, 4, 4), OUT + INP)
    return jax.shard_map(
        shards,
        mesh=split,
        in_specs=(P(OUT, INP), P(INP, OUT), P(INP, OUT), P(OUT, INP)),
        out_specs=P(OUT, INP),
        check_vma=False,
    )
```

```python
import jax
import jax.numpy as jnp
from jax import lax
from jax.experimental import pallas as pl
from jax.experimental.pallas import tpu as pltpu
from jax.sharding import Mesh, PartitionSpec as P

SEQS = 2
SEQ_LEN = 512
OUT = ("z", "ylo", "core")
INP = ("x", "yhi")
CHIPS = ("z", "ylo")
BF16 = jnp.bfloat16
F32 = jnp.float32
ANY = pl.BlockSpec(memory_space=pl.ANY)
VMEM = pl.BlockSpec(memory_space=pltpu.VMEM)


def kernel_call(body, shapes, args, flops=0, unread=0):
    moved = sum(a.size * a.dtype.itemsize for a in args) + sum(s.size * s.dtype.itemsize for s in shapes)
    many = len(shapes) > 1
    return pl.pallas_call(
        body,
        out_shape=shapes if many else shapes[0],
        in_specs=[VMEM] * (len(args) - unread) + [ANY] * unread,
        out_specs=[VMEM] * len(shapes) if many else VMEM,
        compiler_params=pltpu.CompilerParams(vmem_limit_bytes=40 * 2**20),
        cost_estimate=pl.CostEstimate(flops=flops, bytes_accessed=moved, transcendentals=0),
    )(*args)


def swap(value, axis, flip):
    size = lax.axis_size(axis)
    return lax.ppermute(value, axis, [(s, s ^ flip) for s in range(size)])


def gather_yhi(mine):
    return [mine, swap(mine, "yhi", 1), swap(mine, "yhi", 2), swap(mine, "yhi", 3)]


def stack_acts_kernel(block0, block1, block2, block3, order, out):
    rows, features = block0.shape[0], out.shape[2]
    for index, block in enumerate((block0, block1, block2, block3)):
        for side in range(2):
            out[side, index * rows:(index + 1) * rows, :] = block[:, side * features:(side + 1) * features]


def stack_kernel(block0, block1, block2, block3, out):
    rows = block0.shape[0]
    for index, block in enumerate((block0, block1, block2, block3)):
        out[index * rows:(index + 1) * rows, :] = block[...]


def act_dot_kernel(act0, act1, low2, high2, act3, basis0, basis1, out, done):
    first = [act0[0], act1[0], low2[...], act3[0]]
    second = [act0[1], act1[1], high2[...], act3[1]]
    total = 0.0
    for rows, basis in ((first, basis0), (second, basis1)):
        total += jnp.dot(jnp.concatenate(rows), basis[...], preferred_element_type=F32)
    out[...] = total.astype(BF16).reshape(out.shape)
    done[...] = jnp.zeros_like(done)


def grad_dot_kernel(rows, own, other, order, out):
    columns = own.shape[1]
    total = jnp.concatenate(
        [jnp.dot(rows[...], basis[...], preferred_element_type=F32) for basis in (own, other)], axis=1
    )
    out[...] = total.astype(BF16).reshape(out.shape)


def sum_parts(parts):
    total = parts[0].astype(F32)
    for index in range(1, parts.shape[0]):
        total += parts[index].astype(F32)
    return total.astype(BF16)


def sum_copies_kernel(parts, out):
    rounded = sum_parts(parts)
    for index in range(out.shape[0]):
        out[index] = rounded


def sum_split_kernel(done, parts, mine, give):
    rounded = sum_parts(parts)
    columns = mine.shape[1]
    mine[...] = rounded[:, :columns]
    give[...] = rounded[:, columns:]


def square_kernel(g0, g1, g2, g3, act_mine, act_theirs, out):
    columns = out.shape[0]
    half = act_mine.shape[0] // SEQS
    grads = (jnp.concatenate([g0[...], g1[...]]), jnp.concatenate([g2[...], g3[...]]))
    total = 0.0
    for seq in range(SEQS):
        rows = slice(seq * half, (seq + 1) * half)
        contract = (((0,), (0,)), ((), ()))
        rotated = lax.dot_general(grads[seq][:, :columns], act_mine[rows, :], contract, preferred_element_type=F32)
        rotated += lax.dot_general(grads[seq][:, columns:], act_theirs[rows, :], contract, preferred_element_type=F32)
        total = total + rotated * rotated
    out[...] = total * (1.0 / (SEQS * SEQ_LEN))


def both(index, own, other):
    return jnp.where(index == 0, own, other), jnp.where(index == 0, other, own)


def shards(grads, acts, grad_basis, act_basis):
    core = lax.axis_index("core")
    half, features = acts.shape[0] // 2, acts.shape[1]
    tokens, eig = 16 * half, act_basis.shape[1]
    rows, columns = grads.shape[0], grad_basis.shape[1]

    keep = lax.dynamic_slice_in_dim(acts, core * half, half)
    give = lax.dynamic_slice_in_dim(acts, (1 - core) * half, half)
    act_own = jnp.concatenate(both(core, keep, swap(give, "core", 1)), axis=1)
    act_basis0, act_basis1 = both(core, act_basis, swap(act_basis, "core", 1))
    grad_basis_other = swap(grad_basis, "core", 1)

    grad_copies = jnp.broadcast_to(grads[None], (16, *grads.shape))
    grad_rows = lax.all_to_all(grad_copies, CHIPS, 0, 0, tiled=True).reshape(tokens, -1)
    act0 = kernel_call(
        stack_acts_kernel,
        [jax.ShapeDtypeStruct((2, 4 * half, features), BF16)],
        [*gather_yhi(act_own), grad_rows],
        unread=1,
    )
    act1, act3 = swap(act0, "x", 1), swap(act0, "x", 3)
    low2, high2 = swap(act3[0], "x", 1), swap(act1[1], "x", 3)

    grad_partial = kernel_call(
        grad_dot_kernel,
        [jax.ShapeDtypeStruct((16, rows, 2 * columns), BF16)],
        [grad_rows, grad_basis, grad_basis_other, act1],
        flops=2 * tokens * grads.shape[1] * 2 * columns,
        unread=1,
    )
    grad_parts = lax.all_to_all(grad_partial, INP, 0, 0, tiled=True)

    blocks = jax.ShapeDtypeStruct((16, half, eig), BF16)
    act_partial, done = kernel_call(
        act_dot_kernel,
        [blocks, jax.ShapeDtypeStruct((8, 128), F32)],
        [act0, act1, low2, high2, act3, act_basis0, act_basis1],
        flops=2 * tokens * 2 * features * eig,
    )
    act_parts = lax.all_to_all(act_partial, CHIPS, 0, 0, tiled=True)

    narrow = jax.ShapeDtypeStruct((rows, columns), BF16)
    grad_mine, grad_give = kernel_call(sum_split_kernel, [narrow, narrow], [done, grad_parts])
    grad_own = jnp.concatenate([grad_mine, swap(grad_give, "core", 1)], axis=1)
    g0 = kernel_call(stack_kernel, [jax.ShapeDtypeStruct((4 * rows, 2 * columns), BF16)], gather_yhi(grad_own))
    act_parts, g0 = lax.optimization_barrier((act_parts, g0))

    act_mine = lax.all_to_all(kernel_call(sum_copies_kernel, [blocks], [act_parts]), CHIPS, 0, 0, tiled=True)
    g1, g2, g3 = swap(g0, "x", 1), swap(g0, "x", 2), swap(g0, "x", 3)
    act_mine, g1, g2, g3 = lax.optimization_barrier((act_mine.reshape(tokens, eig), g1, g2, g3))
    act_theirs = swap(act_mine, "core", 1)

    return kernel_call(
        square_kernel,
        [jax.ShapeDtypeStruct((columns, eig), F32)],
        [g0, g1, g2, g3, act_mine, act_theirs],
        flops=2 * 2 * tokens * columns * eig,
    )


def solution(mesh):
    split = Mesh(mesh.devices.reshape(8, 2, 2, 4, 4), OUT + INP)
    return jax.shard_map(
        shards,
        mesh=split,
        in_specs=(P(OUT, INP), P(INP, OUT), P(INP, OUT), P(OUT, INP)),
        out_specs=P(OUT, INP),
        check_vma=False,
    )
```

```python
import jax
import jax.numpy as jnp
from jax import lax
from jax.experimental import pallas as pl
from jax.experimental.pallas import tpu as pltpu
from jax.sharding import Mesh, PartitionSpec as P

SEQS = 2
SEQ_LEN = 512
OUT = ("z", "ylo", "core")
INP = ("x", "yhi")
CHIPS = ("z", "ylo")
BF16 = jnp.bfloat16
F32 = jnp.float32
ANY = pl.BlockSpec(memory_space=pl.ANY)
VMEM = pl.BlockSpec(memory_space=pltpu.VMEM)


def kernel_call(body, shapes, args, flops=0, unread=0):
    moved = sum(a.size * a.dtype.itemsize for a in args) + sum(s.size * s.dtype.itemsize for s in shapes)
    many = len(shapes) > 1
    return pl.pallas_call(
        body,
        out_shape=shapes if many else shapes[0],
        in_specs=[VMEM] * (len(args) - unread) + [ANY] * unread,
        out_specs=[VMEM] * len(shapes) if many else VMEM,
        compiler_params=pltpu.CompilerParams(vmem_limit_bytes=40 * 2**20),
        cost_estimate=pl.CostEstimate(flops=flops, bytes_accessed=moved, transcendentals=0),
    )(*args)


def swap(value, axis, flip):
    size = lax.axis_size(axis)
    return lax.ppermute(value, axis, [(s, s ^ flip) for s in range(size)])


def gather_yhi(mine):
    return [mine, swap(mine, "yhi", 1), swap(mine, "yhi", 2), swap(mine, "yhi", 3)]


def stack_acts_kernel(block0, block1, low2, high2, block3, order, out0, out1):
    features, row = out0.shape[1], 0
    for block in (block0, block1, low2, high2, block3):
        rows = block.shape[0]
        for side, out in enumerate((out0, out1)):
            out[row:row + rows, :] = block[:, side * features:(side + 1) * features]
        row += rows


def stack_kernel(block0, block1, block2, block3, out):
    rows = block0.shape[0]
    for index, block in enumerate((block0, block1, block2, block3)):
        out[index * rows:(index + 1) * rows, :] = block[...]


def act_dot_kernel(own0, own1, near0, near1, low2, high2, back0, back1, basis0, basis1, out, done):
    first = [own0[...], near0[...], low2[...], back0[...]]
    second = [own1[...], near1[...], high2[...], back1[...]]
    total = 0.0
    for rows, basis in ((first, basis0), (second, basis1)):
        total += jnp.dot(jnp.concatenate(rows), basis[...], preferred_element_type=F32)
    out[...] = total.astype(BF16).reshape(out.shape)
    done[...] = jnp.zeros_like(done)


def grad_dot_kernel(rows, own, other, order, out):
    columns = own.shape[1]
    total = jnp.concatenate(
        [jnp.dot(rows[...], basis[...], preferred_element_type=F32) for basis in (own, other)], axis=1
    )
    out[...] = total.astype(BF16).reshape(out.shape)


def sum_parts(parts):
    total = parts[0].astype(F32)
    for index in range(1, parts.shape[0]):
        total += parts[index].astype(F32)
    return total.astype(BF16)


def sum_copies_kernel(parts, out):
    rounded = sum_parts(parts)
    for index in range(out.shape[0]):
        out[index] = rounded


def sum_split_kernel(done, parts, mine, give):
    rounded = sum_parts(parts)
    columns = mine.shape[1]
    mine[...] = rounded[:, :columns]
    give[...] = rounded[:, columns:]


def square_kernel(g0, g1, g2, g3, act_mine, act_theirs, out):
    columns = out.shape[0]
    half = act_mine.shape[0] // SEQS
    grads = (jnp.concatenate([g0[...], g1[...]]), jnp.concatenate([g2[...], g3[...]]))
    total = 0.0
    for seq in range(SEQS):
        rows = slice(seq * half, (seq + 1) * half)
        contract = (((0,), (0,)), ((), ()))
        rotated = lax.dot_general(grads[seq][:, :columns], act_mine[rows, :], contract, preferred_element_type=F32)
        rotated += lax.dot_general(grads[seq][:, columns:], act_theirs[rows, :], contract, preferred_element_type=F32)
        total = total + rotated * rotated
    out[...] = total * (1.0 / (SEQS * SEQ_LEN))


def both(index, own, other):
    return jnp.where(index == 0, own, other), jnp.where(index == 0, other, own)


def shards(grads, acts, grad_basis, act_basis):
    core = lax.axis_index("core")
    half, features = acts.shape[0] // 2, acts.shape[1]
    tokens, eig = 16 * half, act_basis.shape[1]
    rows, columns = grads.shape[0], grad_basis.shape[1]

    keep = lax.dynamic_slice_in_dim(acts, core * half, half)
    give = lax.dynamic_slice_in_dim(acts, (1 - core) * half, half)
    act_own = jnp.concatenate(both(core, keep, swap(give, "core", 1)), axis=1)
    act_basis0, act_basis1 = both(core, act_basis, swap(act_basis, "core", 1))
    grad_basis_other = swap(grad_basis, "core", 1)

    grad_copies = jnp.broadcast_to(grads[None], (16, *grads.shape))
    grad_rows = lax.all_to_all(grad_copies, CHIPS, 0, 0, tiled=True).reshape(tokens, -1)
    near, back = swap(act_own, "yhi", 1), swap(act_own, "yhi", 3)
    low, high = swap(back[:half // 2], "yhi", 1), swap(near[half // 2:], "yhi", 3)
    own0, own1 = kernel_call(
        stack_acts_kernel,
        [jax.ShapeDtypeStruct((4 * half, features), BF16)] * 2,
        [act_own, near, low, high, back, grad_rows],
        unread=1,
    )
    near1, back0 = swap(own1, "x", 1), swap(own0, "x", 3)
    low2, high2 = swap(back0, "x", 1), swap(near1, "x", 3)
    near0, back1 = swap(own0, "x", 1), swap(own1, "x", 3)

    grad_partial = kernel_call(
        grad_dot_kernel,
        [jax.ShapeDtypeStruct((16, rows, 2 * columns), BF16)],
        [grad_rows, grad_basis, grad_basis_other, near1],
        flops=2 * tokens * grads.shape[1] * 2 * columns,
        unread=1,
    )
    grad_parts = lax.all_to_all(grad_partial, INP, 0, 0, tiled=True)

    blocks = jax.ShapeDtypeStruct((16, half, eig), BF16)
    act_partial, done = kernel_call(
        act_dot_kernel,
        [blocks, jax.ShapeDtypeStruct((8, 128), F32)],
        [own0, own1, near0, near1, low2, high2, back0, back1, act_basis0, act_basis1],
        flops=2 * tokens * 2 * features * eig,
    )
    act_parts = lax.all_to_all(act_partial, CHIPS, 0, 0, tiled=True)

    narrow = jax.ShapeDtypeStruct((rows, columns), BF16)
    grad_mine, grad_give = kernel_call(sum_split_kernel, [narrow, narrow], [done, grad_parts])
    grad_own = jnp.concatenate([grad_mine, swap(grad_give, "core", 1)], axis=1)
    g0 = kernel_call(stack_kernel, [jax.ShapeDtypeStruct((4 * rows, 2 * columns), BF16)], gather_yhi(grad_own))
    act_parts, g0 = lax.optimization_barrier((act_parts, g0))

    act_mine = lax.all_to_all(kernel_call(sum_copies_kernel, [blocks], [act_parts]), CHIPS, 0, 0, tiled=True)
    g1, g2, g3 = swap(g0, "x", 1), swap(g0, "x", 2), swap(g0, "x", 3)
    act_mine, g1, g2, g3 = lax.optimization_barrier((act_mine.reshape(tokens, eig), g1, g2, g3))
    act_theirs = swap(act_mine, "core", 1)

    return kernel_call(
        square_kernel,
        [jax.ShapeDtypeStruct((columns, eig), F32)],
        [g0, g1, g2, g3, act_mine, act_theirs],
        flops=2 * 2 * tokens * columns * eig,
    )


def solution(mesh):
    split = Mesh(mesh.devices.reshape(8, 2, 2, 4, 4), OUT + INP)
    return jax.shard_map(
        shards,
        mesh=split,
        in_specs=(P(OUT, INP), P(INP, OUT), P(INP, OUT), P(OUT, INP)),
        out_specs=P(OUT, INP),
        check_vma=False,
    )
```

```python
import jax
import jax.numpy as jnp
from jax import lax
from jax.experimental import pallas as pl
from jax.experimental.pallas import tpu as pltpu
from jax.sharding import Mesh, PartitionSpec as P

SEQS = 2
SEQ_LEN = 512
OUT = ("z", "ylo", "core")
INP = ("x", "yhi")
CHIPS = ("z", "ylo")
BF16 = jnp.bfloat16
F32 = jnp.float32
ANY = pl.BlockSpec(memory_space=pl.ANY)
VMEM = pl.BlockSpec(memory_space=pltpu.VMEM)


def kernel_call(body, shapes, args, flops=0, unread=0):
    moved = sum(a.size * a.dtype.itemsize for a in args) + sum(s.size * s.dtype.itemsize for s in shapes)
    many = len(shapes) > 1
    return pl.pallas_call(
        body,
        out_shape=shapes if many else shapes[0],
        in_specs=[VMEM] * (len(args) - unread) + [ANY] * unread,
        out_specs=[VMEM] * len(shapes) if many else VMEM,
        compiler_params=pltpu.CompilerParams(vmem_limit_bytes=40 * 2**20),
        cost_estimate=pl.CostEstimate(flops=flops, bytes_accessed=moved, transcendentals=0),
    )(*args)


def swap(value, axis, flip):
    size = lax.axis_size(axis)
    return lax.ppermute(value, axis, [(s, s ^ flip) for s in range(size)])


def gather_yhi(mine):
    return [mine, swap(mine, "yhi", 1), swap(mine, "yhi", 2), swap(mine, "yhi", 3)]


def copies_kernel(block, order, out):
    for index in range(out.shape[0]):
        out[index] = block[...]


def stack_acts_kernel(block0, block1, block2, block3, order, out):
    rows, features = block0.shape[0], out.shape[2]
    for index, block in enumerate((block0, block1, block2, block3)):
        for side in range(2):
            out[side, index * rows:(index + 1) * rows, :] = block[:, side * features:(side + 1) * features]


def stack_kernel(block0, block1, block2, block3, out):
    rows = block0.shape[0]
    for index, block in enumerate((block0, block1, block2, block3)):
        out[index * rows:(index + 1) * rows, :] = block[...]


def act_dot_kernel(act0, act1, low2, high2, act3, basis0, basis1, out, done):
    first = [act0[0], act1[0], low2[...], act3[0]]
    second = [act0[1], act1[1], high2[...], act3[1]]
    total = 0.0
    for rows, basis in ((first, basis0), (second, basis1)):
        total += jnp.dot(jnp.concatenate(rows), basis[...], preferred_element_type=F32)
    out[...] = total.astype(BF16).reshape(out.shape)
    done[...] = jnp.zeros_like(done)


def grad_dot_kernel(rows, own, other, order, out):
    columns = own.shape[1]
    total = jnp.concatenate(
        [jnp.dot(rows[...], basis[...], preferred_element_type=F32) for basis in (own, other)], axis=1
    )
    out[...] = total.astype(BF16).reshape(out.shape)


def sum_parts(parts):
    total = parts[0].astype(F32)
    for index in range(1, parts.shape[0]):
        total += parts[index].astype(F32)
    return total.astype(BF16)


def sum_copies_kernel(parts, out):
    rounded = sum_parts(parts)
    for index in range(out.shape[0]):
        out[index] = rounded


def sum_split_kernel(done, parts, mine, give):
    rounded = sum_parts(parts)
    columns = mine.shape[1]
    mine[...] = rounded[:, :columns]
    give[...] = rounded[:, columns:]


def square_kernel(g0, g1, g2, g3, act_mine, act_theirs, out):
    columns = out.shape[0]
    half = act_mine.shape[0] // SEQS
    grads = (jnp.concatenate([g0[...], g1[...]]), jnp.concatenate([g2[...], g3[...]]))
    total = 0.0
    for seq in range(SEQS):
        rows = slice(seq * half, (seq + 1) * half)
        contract = (((0,), (0,)), ((), ()))
        rotated = lax.dot_general(grads[seq][:, :columns], act_mine[rows, :], contract, preferred_element_type=F32)
        rotated += lax.dot_general(grads[seq][:, columns:], act_theirs[rows, :], contract, preferred_element_type=F32)
        total = total + rotated * rotated
    out[...] = total * (1.0 / (SEQS * SEQ_LEN))


def both(index, own, other):
    return jnp.where(index == 0, own, other), jnp.where(index == 0, other, own)


def shards(grads, acts, grad_basis, act_basis):
    core = lax.axis_index("core")
    half, features = acts.shape[0] // 2, acts.shape[1]
    tokens, eig = 16 * half, act_basis.shape[1]
    rows, columns = grads.shape[0], grad_basis.shape[1]

    keep = lax.dynamic_slice_in_dim(acts, core * half, half)
    give = lax.dynamic_slice_in_dim(acts, (1 - core) * half, half)
    act_own = jnp.concatenate(both(core, keep, swap(give, "core", 1)), axis=1)
    act_basis0, act_basis1 = both(core, act_basis, swap(act_basis, "core", 1))
    grad_basis_other = swap(grad_basis, "core", 1)

    grad_copies = kernel_call(
        copies_kernel, [jax.ShapeDtypeStruct((16, *grads.shape), BF16)], [grads, act_own], unread=1
    )
    grad_rows = lax.all_to_all(grad_copies, CHIPS, 0, 0, tiled=True).reshape(tokens, -1)
    act0 = kernel_call(
        stack_acts_kernel,
        [jax.ShapeDtypeStruct((2, 4 * half, features), BF16)],
        [*gather_yhi(act_own), grad_rows],
        unread=1,
    )
    act1, act3 = swap(act0, "x", 1), swap(act0, "x", 3)
    low2, high2 = swap(act3[0], "x", 1), swap(act1[1], "x", 3)

    grad_partial = kernel_call(
        grad_dot_kernel,
        [jax.ShapeDtypeStruct((16, rows, 2 * columns), BF16)],
        [grad_rows, grad_basis, grad_basis_other, act1],
        flops=2 * tokens * grads.shape[1] * 2 * columns,
        unread=1,
    )
    grad_parts = lax.all_to_all(grad_partial, INP, 0, 0, tiled=True)

    blocks = jax.ShapeDtypeStruct((16, half, eig), BF16)
    act_partial, done = kernel_call(
        act_dot_kernel,
        [blocks, jax.ShapeDtypeStruct((8, 128), F32)],
        [act0, act1, low2, high2, act3, act_basis0, act_basis1],
        flops=2 * tokens * 2 * features * eig,
    )
    act_parts = lax.all_to_all(act_partial, CHIPS, 0, 0, tiled=True)

    narrow = jax.ShapeDtypeStruct((rows, columns), BF16)
    grad_mine, grad_give = kernel_call(sum_split_kernel, [narrow, narrow], [done, grad_parts])
    grad_own = jnp.concatenate([grad_mine, swap(grad_give, "core", 1)], axis=1)
    g0 = kernel_call(stack_kernel, [jax.ShapeDtypeStruct((4 * rows, 2 * columns), BF16)], gather_yhi(grad_own))
    act_parts, g0 = lax.optimization_barrier((act_parts, g0))

    act_mine = lax.all_to_all(kernel_call(sum_copies_kernel, [blocks], [act_parts]), CHIPS, 0, 0, tiled=True)
    g1, g2, g3 = swap(g0, "x", 1), swap(g0, "x", 2), swap(g0, "x", 3)
    act_mine, g1, g2, g3 = lax.optimization_barrier((act_mine.reshape(tokens, eig), g1, g2, g3))
    act_theirs = swap(act_mine, "core", 1)

    return kernel_call(
        square_kernel,
        [jax.ShapeDtypeStruct((columns, eig), F32)],
        [g0, g1, g2, g3, act_mine, act_theirs],
        flops=2 * 2 * tokens * columns * eig,
    )


def solution(mesh):
    split = Mesh(mesh.devices.reshape(8, 2, 2, 4, 4), OUT + INP)
    return jax.shard_map(
        shards,
        mesh=split,
        in_specs=(P(OUT, INP), P(INP, OUT), P(INP, OUT), P(OUT, INP)),
        out_specs=P(OUT, INP),
        check_vma=False,
    )
```

```python
import jax
import jax.numpy as jnp
from jax import lax
from jax.experimental import pallas as pl
from jax.experimental.pallas import tpu as pltpu
from jax.sharding import Mesh, PartitionSpec as P

SEQS = 2
SEQ_LEN = 512
OUT = ("z", "ylo", "core")
INP = ("x", "yhi")
CHIPS = ("z", "ylo")
BF16 = jnp.bfloat16
F32 = jnp.float32
ANY = pl.BlockSpec(memory_space=pl.ANY)
VMEM = pl.BlockSpec(memory_space=pltpu.VMEM)


def kernel_call(body, shapes, args, flops=0, unread=0):
    moved = sum(a.size * a.dtype.itemsize for a in args) + sum(s.size * s.dtype.itemsize for s in shapes)
    many = len(shapes) > 1
    return pl.pallas_call(
        body,
        out_shape=shapes if many else shapes[0],
        in_specs=[VMEM] * (len(args) - unread) + [ANY] * unread,
        out_specs=[VMEM] * len(shapes) if many else VMEM,
        compiler_params=pltpu.CompilerParams(vmem_limit_bytes=40 * 2**20),
        cost_estimate=pl.CostEstimate(flops=flops, bytes_accessed=moved, transcendentals=0),
    )(*args)


def swap(value, axis, flip):
    size = lax.axis_size(axis)
    return lax.ppermute(value, axis, [(s, s ^ flip) for s in range(size)])


def gather_yhi(mine):
    return [mine, swap(mine, "yhi", 1), swap(mine, "yhi", 2), swap(mine, "yhi", 3)]


def copies_kernel(block, order, out):
    for index in range(out.shape[0]):
        out[index] = block[...]


def stack_acts_kernel(block0, block1, block2, block3, out):
    rows, features = block0.shape[0], out.shape[2]
    for index, block in enumerate((block0, block1, block2, block3)):
        for side in range(2):
            out[side, index * rows:(index + 1) * rows, :] = block[:, side * features:(side + 1) * features]


def stack_kernel(block0, block1, block2, block3, out):
    rows = block0.shape[0]
    for index, block in enumerate((block0, block1, block2, block3)):
        out[index * rows:(index + 1) * rows, :] = block[...]


def act_dot_kernel(act0, act1, low2, high2, act3, basis0, basis1, out, done):
    first = [act0[0], act1[0], low2[...], act3[0]]
    second = [act0[1], act1[1], high2[...], act3[1]]
    total = 0.0
    for rows, basis in ((first, basis0), (second, basis1)):
        total += jnp.dot(jnp.concatenate(rows), basis[...], preferred_element_type=F32)
    out[...] = total.astype(BF16).reshape(out.shape)
    done[...] = jnp.zeros_like(done)


def grad_dot_kernel(rows, own, other, order, out):
    columns = own.shape[1]
    total = jnp.concatenate(
        [jnp.dot(rows[...], basis[...], preferred_element_type=F32) for basis in (own, other)], axis=1
    )
    out[...] = total.astype(BF16).reshape(out.shape)


def sum_parts(parts):
    total = parts[0].astype(F32)
    for index in range(1, parts.shape[0]):
        total += parts[index].astype(F32)
    return total.astype(BF16)


def sum_copies_kernel(parts, out):
    rounded = sum_parts(parts)
    for index in range(out.shape[0]):
        out[index] = rounded


def sum_split_kernel(done, parts, mine, give):
    rounded = sum_parts(parts)
    columns = mine.shape[1]
    mine[...] = rounded[:, :columns]
    give[...] = rounded[:, columns:]


def square_kernel(g0, g1, g2, g3, act_mine, act_theirs, out):
    columns = out.shape[0]
    half = act_mine.shape[0] // SEQS
    grads = (jnp.concatenate([g0[...], g1[...]]), jnp.concatenate([g2[...], g3[...]]))
    total = 0.0
    for seq in range(SEQS):
        rows = slice(seq * half, (seq + 1) * half)
        contract = (((0,), (0,)), ((), ()))
        rotated = lax.dot_general(grads[seq][:, :columns], act_mine[rows, :], contract, preferred_element_type=F32)
        rotated += lax.dot_general(grads[seq][:, columns:], act_theirs[rows, :], contract, preferred_element_type=F32)
        total = total + rotated * rotated
    out[...] = total * (1.0 / (SEQS * SEQ_LEN))


def both(index, own, other):
    return jnp.where(index == 0, own, other), jnp.where(index == 0, other, own)


def shards(grads, acts, grad_basis, act_basis):
    core = lax.axis_index("core")
    half, features = acts.shape[0] // 2, acts.shape[1]
    tokens, eig = 16 * half, act_basis.shape[1]
    rows, columns = grads.shape[0], grad_basis.shape[1]

    keep = lax.dynamic_slice_in_dim(acts, core * half, half)
    give = lax.dynamic_slice_in_dim(acts, (1 - core) * half, half)
    act_own = jnp.concatenate(both(core, keep, swap(give, "core", 1)), axis=1)
    act_basis0, act_basis1 = both(core, act_basis, swap(act_basis, "core", 1))
    grad_basis_other = swap(grad_basis, "core", 1)

    grad_copies = kernel_call(
        copies_kernel, [jax.ShapeDtypeStruct((16, *grads.shape), BF16)], [grads, act_own], unread=1
    )
    grad_rows = lax.all_to_all(grad_copies, CHIPS, 0, 0, tiled=True).reshape(tokens, -1)
    act0 = kernel_call(
        stack_acts_kernel,
        [jax.ShapeDtypeStruct((2, 4 * half, features), BF16)],
        gather_yhi(act_own),
    )
    act1, act3 = swap(act0, "x", 1), swap(act0, "x", 3)
    low2, high2 = swap(act3[0], "x", 1), swap(act1[1], "x", 3)

    grad_partial = kernel_call(
        grad_dot_kernel,
        [jax.ShapeDtypeStruct((16, rows, 2 * columns), BF16)],
        [grad_rows, grad_basis, grad_basis_other, act1],
        flops=2 * tokens * grads.shape[1] * 2 * columns,
        unread=1,
    )
    grad_parts = lax.all_to_all(grad_partial, INP, 0, 0, tiled=True)

    blocks = jax.ShapeDtypeStruct((16, half, eig), BF16)
    act_partial, done = kernel_call(
        act_dot_kernel,
        [blocks, jax.ShapeDtypeStruct((8, 128), F32)],
        [act0, act1, low2, high2, act3, act_basis0, act_basis1],
        flops=2 * tokens * 2 * features * eig,
    )
    act_parts = lax.all_to_all(act_partial, CHIPS, 0, 0, tiled=True)

    narrow = jax.ShapeDtypeStruct((rows, columns), BF16)
    grad_mine, grad_give = kernel_call(sum_split_kernel, [narrow, narrow], [done, grad_parts])
    grad_own = jnp.concatenate([grad_mine, swap(grad_give, "core", 1)], axis=1)
    g0 = kernel_call(stack_kernel, [jax.ShapeDtypeStruct((4 * rows, 2 * columns), BF16)], gather_yhi(grad_own))
    act_parts, g0 = lax.optimization_barrier((act_parts, g0))

    act_mine = lax.all_to_all(kernel_call(sum_copies_kernel, [blocks], [act_parts]), CHIPS, 0, 0, tiled=True)
    g1, g2, g3 = swap(g0, "x", 1), swap(g0, "x", 2), swap(g0, "x", 3)
    act_mine, g1, g2, g3 = lax.optimization_barrier((act_mine.reshape(tokens, eig), g1, g2, g3))
    act_theirs = swap(act_mine, "core", 1)

    return kernel_call(
        square_kernel,
        [jax.ShapeDtypeStruct((columns, eig), F32)],
        [g0, g1, g2, g3, act_mine, act_theirs],
        flops=2 * 2 * tokens * columns * eig,
    )


def solution(mesh):
    split = Mesh(mesh.devices.reshape(8, 2, 2, 4, 4), OUT + INP)
    return jax.shard_map(
        shards,
        mesh=split,
        in_specs=(P(OUT, INP), P(INP, OUT), P(INP, OUT), P(OUT, INP)),
        out_specs=P(OUT, INP),
        check_vma=False,
    )
```
